32 devices in a mesh: groups: 2 (over x), wide: 16 (over z, y, core).
Axes of the slice: x: 2, y: 2, z: 4, core: 2. Of those that a mesh axis runs over, the one named last changes fastest.
Arguments:
- features: bfloat16 [32768, 128], P(('groups', 'wide')), parts along dimension 0, may hold values from -6 to 6
- fetch_ids: int32 [32, 16, 16], P('groups', 'wide'), parts along dimension 0, may hold values from 0 to 1023
- tile_lists: int32 [512, 64], P(('groups', 'wide')), parts along dimension 0, may hold values from 0 to 255
- depth_order: int32 [512, 64], P(('groups', 'wide')), parts along dimension 0, may hold values from 0 to 63, each once within a row
- alpha_codes: int32 [512, 64, 256], P(('groups', 'wide')), parts along dimension 0, may hold values from 0 to 255
- list_counts: int32 [32, 16], P(('groups', 'wide')), parts along dimension 0, may hold values from 1 to 64, 544 in all within a row
- targets: bfloat16 [131072, 1024], P(('groups', 'wide')), parts along dimension 0, may hold values from -6 to 6
- dec_weight: bfloat16 [128, 1024], replicated, may hold values from -0.5 to 0.5
Outputs:
- feat_grad: float32 [32768, 128], P(('groups', 'wide')), parts along dimension 0
- dec_grad: float32 [256, 1024], P(('groups', 'wide')), parts along dimension 0
- loss: float32 [2], P('groups'), parts along dimension 0
The draws below stay inside these ranges and needn't reach their ends.
There are 2 independent parts, one for each index of `groups`. The reference program is written for one: setup_inputs(seed, part) draws one part's arguments, and reference() takes and returns one part's arrays. A program takes and returns all parts, laid end to end along the dimension named above; an argument that names none is the same for every part. Nothing has to cross between parts.
All inputs are finite; a program needn't handle non-finite values.
Results may differ from the reference program's by a relative error of at most 0.0011.
Values may be sent and summed in bfloat16 or wider, within the bound.
No kernel may reach another device: no remote copies, remote signals or barrier semaphores. Data moves between devices by JAX's collectives and lax.ppermute only.
A program may use at most 128 MiB of HBM per device.

```python
import math
import jax
import jax.numpy as jnp
import numpy as np
from jax import lax

FEAT = 128
C_DEC = 1024
PIX = 256
LIST = 64
CAP = 16
G_DEV = 1024
TILE_DEV = 16
GAUSS = 16384
TILES = 256
PIXELS = 65536
N_WIDE = 16


def plant(entries, own_key, smallest, high):
    index_at = [jax.random.randint(jax.random.fold_in(own_key, axis), (), 0, length) for axis, length in enumerate(entries.shape)]
    widest = entries.shape.index(max(entries.shape))
    next_to = index_at[:widest] + [(index_at[widest] + 1) % entries.shape[widest]] + index_at[widest + 1:]
    return entries.at[tuple(index_at)].set(smallest).at[tuple(next_to)].set(high)


def steps_of(rng, dims, cuts, least, top_value):
    def one(dim, parts):
        heights = jax.random.uniform(jax.random.fold_in(jax.random.fold_in(rng, 6), dim), (parts,), jnp.float32, least / len(cuts), top_value / len(cuts))
        return jnp.repeat(jnp.exp(heights), dims[dim] // parts).reshape((-1,) + (1,) * (len(dims) - dim - 1))

    loudness = one(*cuts[0])
    for cut in cuts[1:]:
        loudness = loudness * one(*cut)
    return loudness


def profile(number_of, total, reach, slope):
    weights = [(1 << 20) // math.isqrt(rank ** slope) + 1 for rank in range(2, number_of + 1)]
    spare, holding = total - reach - (number_of - 1), [1] * (number_of - 1)
    while spare > 0:
        free = [i for i in range(number_of - 1) if holding[i] < reach]
        mass, remaining = sum([weights[i] for i in free]), spare
        for i in free:
            addition = min(reach - holding[i], max(1, remaining * weights[i] // mass), spare)
            holding[i] = holding[i] + addition
            spare = spare - addition
    return np.array([reach] + holding)


def uneven(key, count, total, reach, slope):
    if count == 2:
        one = jax.random.randint(key, (), max(1, total - reach), min(reach, total - 1) + 1)
        return jnp.stack([one, total - one])
    lengths = jnp.asarray(profile(count, total, reach, slope), jnp.int32)
    couples = (count - 1) // 2
    donor, sink = lengths[1:1 + 2 * couples:2], lengths[2:2 + 2 * couples:2]
    slack = jnp.minimum(donor - 1, reach - sink)
    moved = jax.random.randint(jax.random.fold_in(key, 1), (couples,), 0, 1 << 20) % (slack + 1)
    lengths = lengths.at[1:1 + 2 * couples:2].set(donor - moved).at[2:2 + 2 * couples:2].set(sink + moved)
    return lengths[jax.random.permutation(jax.random.fold_in(key, 2), count)]


def bell_draw(stream_key, dims, scale, limit, cuts=(), kind=jnp.bfloat16):
    result = scale * jax.random.normal(stream_key, dims, jnp.float32)
    if cuts:
        result = result * steps_of(stream_key, dims, cuts, -0.22, 0.18)
    return jnp.clip(result, -limit, limit).astype(kind)


def setup_inputs(seed: int = 0, part: int = 0) -> dict:
    key_list = jax.random.split(jax.random.key(seed), 9)
    part_splits = jax.random.split(jax.random.fold_in(key_list[8], part), 9)
    features = bell_draw(part_splits[0], (GAUSS, FEAT), 1.0, 6.0, ((0, 16),))
    fetch_ids = plant(jax.random.randint(part_splits[1], (N_WIDE, N_WIDE, CAP), 0, G_DEV), jax.random.fold_in(part_splits[1], 1), 0, G_DEV - 1).astype(jnp.int32)
    tile_lists = plant(jax.random.randint(part_splits[2], (TILES, LIST), 0, N_WIDE * CAP), jax.random.fold_in(part_splits[2], 1), 0, (N_WIDE * CAP) - 1).astype(jnp.int32)
    depth_order = jax.vmap(lambda own: jax.random.permutation(own, LIST))(jax.random.split(part_splits[3], TILES)).reshape((TILES, LIST)).astype(jnp.int32)
    alpha_codes = plant(jax.random.randint(part_splits[4], (TILES, LIST, PIX), 0, 256), jax.random.fold_in(part_splits[4], 1), 0, 255).astype(jnp.int32)
    list_counts = jax.vmap(lambda own: uneven(own, TILE_DEV, TILE_DEV * LIST // 2 + LIST // 2, LIST, 2))(jax.random.split(part_splits[5], N_WIDE)).reshape((N_WIDE, TILE_DEV)).astype(jnp.int32)
    targets = bell_draw(part_splits[6], (PIXELS, C_DEC), 1.0, 6.0, ((0, 16),))
    dec_weight = bell_draw(key_list[7], (FEAT, C_DEC), FEAT ** -0.5, 0.5)
    return {"features": features, "fetch_ids": fetch_ids, "tile_lists": tile_lists, "depth_order": depth_order, "alpha_codes": alpha_codes, "list_counts": list_counts, "targets": targets, "dec_weight": dec_weight}


ALPHA_TOP = 0.1

def render(buffer, tile_lists, depth_order, alpha_codes, list_counts, targets, dec_weight):
    slots = jnp.take_along_axis(tile_lists, depth_order, axis=1)
    ordered = jnp.take_along_axis(alpha_codes, depth_order[:, :, None], axis=1)
    positions = jnp.arange(tile_lists.shape[1], dtype=jnp.int32)
    active = (positions[None, :] < list_counts[:, None]).astype(jnp.float32)
    alpha = ordered.astype(jnp.float32) * (ALPHA_TOP / 255.0) * active[:, :, None]
    through = jnp.cumprod(1.0 - alpha, axis=1)
    transmit = jnp.concatenate([jnp.ones_like(through[:, :1]), through[:, :-1]], axis=1)
    blend = (transmit * alpha).astype(jnp.bfloat16)
    gathered = buffer[slots]
    composite = jnp.einsum('tkp,tkf->tpf', blend.astype(jnp.float32), gathered.astype(jnp.float32))
    composite = composite.astype(jnp.bfloat16).reshape(-1, buffer.shape[1])
    decoded = jnp.dot(composite, dec_weight, preferred_element_type=jnp.float32)
    residual = decoded - targets.astype(jnp.float32)
    loss_part = jnp.sum(residual * residual)
    grad_out = residual.astype(jnp.bfloat16)
    weight_term = jnp.dot(composite.T, grad_out, preferred_element_type=jnp.float32)
    grad_comp = jnp.dot(grad_out, dec_weight.T, preferred_element_type=jnp.float32).astype(jnp.bfloat16)
    grad_comp = grad_comp.reshape(blend.shape[0], blend.shape[2], -1)
    grad_slot = jnp.einsum('tkp,tpf->tkf', blend.astype(jnp.float32), grad_comp.astype(jnp.float32))
    grad_buffer = jnp.zeros(buffer.shape, jnp.float32).at[slots.reshape(-1)].add(grad_slot.reshape(-1, buffer.shape[1]))
    return (weight_term, loss_part, grad_buffer)

def reference(features, fetch_ids, tile_lists, depth_order, alpha_codes, list_counts, targets, dec_weight):
    owner_base = (jnp.arange(N_WIDE, dtype=jnp.int32) * G_DEV)[None, :, None]
    global_ids = (fetch_ids + owner_base).reshape(N_WIDE, N_WIDE * CAP).astype(jnp.int32)

    def device_step(inputs):
        row_ids, lists, order, alpha_table, counts, goal = inputs
        buffer = features[row_ids]
        return render(buffer, lists, order, alpha_table, counts, goal, dec_weight)
    terms, losses, grads = lax.map(device_step, (global_ids, tile_lists.reshape(N_WIDE, TILE_DEV, LIST), depth_order.reshape(N_WIDE, TILE_DEV, LIST), alpha_codes.reshape(N_WIDE, TILE_DEV, LIST, PIX), list_counts, targets.reshape(N_WIDE, TILE_DEV * PIX, C_DEC)))
    feat_grad = jnp.zeros((G_DEV * N_WIDE, FEAT), jnp.float32).at[global_ids.reshape(-1)].add(grads.reshape(-1, FEAT))
    dec_grad = lax.optimization_barrier(jnp.sum(terms, axis=0)) * (1.0 / math.sqrt(PIXELS))
    loss = (0.5 * jnp.sum(losses) / (PIXELS * C_DEC)).reshape(1)
    return (feat_grad, dec_grad, loss)
```

```python
import functools
import math

import jax
import jax.numpy as jnp
from jax import lax
from jax.experimental import pallas as pl
from jax.experimental.pallas import tpu as pltpu
from jax.sharding import PartitionSpec as P

ALPHA_TOP = 0.1
NN = (((1,), (0,)), ((), ()))
NT = (((1,), (1,)), ((), ()))
TN = (((0,), (0,)), ((), ()))
VMEM = pl.BlockSpec(memory_space=pltpu.VMEM)
SMEM = pl.BlockSpec(memory_space=pltpu.SMEM)
ANY = pl.BlockSpec(memory_space=pl.ANY)


def dot(a, b, dims=NN):
    return lax.dot_general(a, b, dims, preferred_element_type=jnp.float32)


def split(x):
    high = x.astype(jnp.bfloat16)
    return high, (x - high.astype(jnp.float32)).astype(jnp.bfloat16)


def one_hot(condition):
    return jnp.where(condition, 1.0, 0.0).astype(jnp.bfloat16)


def params(mib):
    return pltpu.CompilerParams(vmem_limit_bytes=mib << 20)


def pick_kernel(request_ref, feature_ref, out_ref):
    rows, owned = request_ref.shape[0], feature_ref.shape[0]
    lane = lax.broadcasted_iota(jnp.int32, (rows, owned), 1)
    chosen = one_hot(request_ref[...] == lane)
    out_ref[...] = dot(chosen, feature_ref[...]).astype(jnp.bfloat16)


def blend_pair(order, codes, count_first, count_second, list_len):
    both = 2 * list_len
    row = lax.broadcasted_iota(jnp.int32, (both, both), 0)
    lane = lax.broadcasted_iota(jnp.int32, (both, both), 1)
    same = (row >= list_len) == (lane >= list_len)
    place = order + jnp.where(lane[:1] >= list_len, list_len, 0)
    at = row == place
    rank = jnp.sum(jnp.where(at, lane.astype(jnp.float32), 0.0), axis=1, keepdims=True)
    ahead = same & (lane.astype(jnp.float32) < rank)
    nearer = dot(one_hot(ahead), one_hot(at), NT).astype(jnp.bfloat16)
    alpha = codes.astype(jnp.float32) * (ALPHA_TOP / 255.0)
    high, low = split(jnp.log(1.0 - alpha))
    transmit = jnp.exp(dot(nearer, high) + dot(nearer, low))
    slot = lax.broadcasted_iota(jnp.int32, (both, 1), 0)
    limit = jnp.where(slot < list_len, count_first, count_second + list_len)
    live = rank < limit.astype(jnp.float32)
    return jnp.where(live, transmit * alpha, 0.0).astype(jnp.bfloat16), same


def gram_kernel(
    count_ref,
    list_ref,
    order_ref,
    weight_ref,
    code_hbm,
    target_hbm,
    gram_high_ref,
    gram_low_ref,
    cross_high_ref,
    cross_low_ref,
    back_ref,
    square_high_ref,
    square_low_ref,
    loss_ref,
    codes,
    target,
    hot,
    part_high,
    part_low,
    blends,
    bt_high,
    bt_low,
    code_sem,
    target_sem,
):
    tiles, list_len, pixels = codes.shape
    rows = gram_high_ref.shape[0]
    both = 2 * list_len
    pairs = tiles // 2
    code_copies = [
        pltpu.make_async_copy(
            code_hbm.at[pl.ds(2 * i, 2)], codes.at[pl.ds(2 * i, 2)], code_sem.at[i]
        )
        for i in range(pairs)
    ]
    target_copies = [
        pltpu.make_async_copy(
            target_hbm.at[pl.ds(t * pixels, pixels)],
            target.at[pl.ds(t * pixels, pixels)],
            target_sem.at[t],
        )
        for t in range(tiles)
    ]
    for copy in code_copies + target_copies:
        copy.start()
    weight = weight_ref[...]
    high, low = split(dot(weight, weight, NT))
    square_high_ref[...] = high
    square_low_ref[...] = low
    for i in range(pairs):
        code_copies[i].wait()
        blend, same = blend_pair(
            order_ref[i : i + 1, :],
            codes[2 * i : 2 * i + 2].reshape(both, pixels),
            count_ref[0, 2 * i],
            count_ref[0, 2 * i + 1],
            list_len,
        )
        own = slice(i * both, (i + 1) * both)
        blends[own, :] = blend
        place = lax.broadcasted_iota(jnp.int32, (rows, both), 0)
        chosen = one_hot(list_ref[i : i + 1, :] == place)
        hot[:, own] = chosen
        high, low = split(jnp.where(same, dot(blend, blend, NT), 0.0))
        high, low = split(dot(chosen, high) + dot(chosen, low))
        part_high[:, own] = high
        part_low[:, own] = low
    total = jnp.zeros((8, target.shape[1]), jnp.float32)
    for t in range(tiles):
        target_copies[t].wait()
        goal = target[t * pixels : (t + 1) * pixels, :]
        own = slice(t * list_len, (t + 1) * list_len)
        high, low = split(dot(blends[own, :], goal))
        bt_high[own, :] = high
        bt_low[own, :] = low
        wide = goal.astype(jnp.float32)
        total = total + jnp.sum((wide * wide).reshape(pixels // 8, 8, -1), axis=0)
    loss_ref[...] = jnp.full(loss_ref.shape, jnp.sum(total), jnp.float32)
    chosen = hot[...]
    high, low = split(dot(part_high[...], chosen, NT) + dot(part_low[...], chosen, NT))
    gram_high_ref[...] = high
    gram_low_ref[...] = low
    high, low = split(dot(chosen, bt_high[...]) + dot(chosen, bt_low[...]))
    cross_high_ref[...] = high
    cross_low_ref[...] = low
    back_ref[...] = dot(high, weight, NT) + dot(low, weight, NT)


def gradient_kernel(
    parity_ref,
    buffer_ref,
    gram_high_ref,
    gram_low_ref,
    cross_high_ref,
    cross_low_ref,
    back_ref,
    square_high_ref,
    square_low_ref,
    loss_ref,
    weight_ref,
    send_ref,
    keep_ref,
    grads,
):
    parity = parity_ref[0]
    buffer = buffer_ref[...]
    rows, channels = buffer.shape
    chunks = send_ref.shape[0]
    per_owner = rows // (2 * chunks)
    share = channels // (2 * chunks)
    lanes = 128
    width = weight_ref.shape[1]
    strips = width // lanes
    body = share * strips
    half = channels // 2
    mixed = dot(gram_high_ref[...], buffer) + dot(gram_low_ref[...], buffer)
    high, low = split(mixed)
    square_high = square_high_ref[...]
    back = back_ref[...]
    slope = dot(high, square_high) + dot(low, square_high) + dot(high, square_low_ref[...]) - back
    grads[...] = slope
    loss = loss_ref[...] + jnp.sum(buffer.astype(jnp.float32) * (slope - back))
    source = lax.broadcasted_iota(jnp.int32, (channels, channels), 0)
    goal = lax.broadcasted_iota(jnp.int32, (channels, channels), 1)
    second = goal >= half
    inner = jnp.where(second, goal - half, goal)
    side = jnp.where(second, parity, 1 - parity)
    chunk = inner // share
    wanted = chunk * (2 * share) + side * share + (inner - chunk * share)
    ordered = dot(buffer, one_hot(source == wanted)).astype(jnp.bfloat16)
    core_high, core_low = split(dot(ordered, high, TN) + dot(ordered, low, TN))
    weight = weight_ref[...]
    grad = dot(core_high, weight) + dot(core_low, weight)
    grad = grad - dot(ordered, cross_high_ref[...], TN) - dot(ordered, cross_low_ref[...], TN)
    for number, (ref, which) in enumerate(((send_ref, 1 - parity), (keep_ref, parity))):
        for i in range(chunks):
            top = number * half + i * share
            for j in range(strips):
                ref[i, j * share : (j + 1) * share, :] = grad[
                    top : top + share, j * lanes : (j + 1) * lanes
                ]
            begin = pl.multiple_of((2 * i + which) * per_owner, per_owner)
            ref[i, body : body + per_owner, :] = grads[pl.ds(begin, per_owner), :]
            ref[i, body + per_owner :, :] = loss


def join_kernel(body, per_owner, keep_ref, got_ref, out_ref):
    out_ref[:, :body, :] = keep_ref[:, :body, :] + got_ref[:, :body, :]
    out_ref[:, body : body + per_owner, :] = keep_ref[:, body : body + per_owner, :]
    out_ref[:, body + per_owner : body + 2 * per_owner, :] = got_ref[:, body : body + per_owner, :]
    out_ref[:, body + 2 * per_owner :, :] = (
        keep_ref[:, body + per_owner :, :] + got_ref[:, body + per_owner :, :]
    )


def finish_kernel(
    body, per_owner, dec_scale, loss_scale, request_ref, got_ref, feat_ref, dec_ref, loss_ref
):
    chunks = got_ref.shape[0]
    owned = feat_ref.shape[0]
    share = dec_ref.shape[0]
    lanes = got_ref.shape[2]
    total = jnp.sum(got_ref[:, :body, :], axis=0) * dec_scale
    for j in range(body // share):
        dec_ref[:, j * lanes : (j + 1) * lanes] = total[j * share : (j + 1) * share, :]
    tail = jnp.sum(got_ref[:, body + 2 * per_owner :, :], axis=0)
    loss_ref[...] = tail[:1, :] * loss_scale
    moved = got_ref[:, body : body + 2 * per_owner, :].reshape(chunks * 2 * per_owner, lanes)
    high, low = split(moved)
    place = lax.broadcasted_iota(jnp.int32, (owned, moved.shape[0]), 0)
    chosen = one_hot(place == request_ref[...])
    feat_ref[...] = dot(chosen, high) + dot(chosen, low)


def local(
    features, fetch_ids, tile_lists, depth_order, alpha_codes, list_counts, targets, dec_weight
):
    f32, bf16 = jnp.float32, jnp.bfloat16
    peers = lax.axis_size("wide")
    owned, channels = features.shape
    per_owner = fetch_ids.shape[2]
    rows = peers * per_owner
    tiles, list_len, pixels = alpha_codes.shape
    width = targets.shape[1]
    slots = tiles * list_len
    chunks = peers // 2
    share = channels // peers
    lanes = 128
    body = share * (width // lanes)
    parity = lax.rem(lax.axis_index("wide"), 2)
    requests = fetch_ids[:, 0, :]
    outgoing = pl.pallas_call(
        pick_kernel,
        out_shape=jax.ShapeDtypeStruct((rows, channels), bf16),
        in_specs=[VMEM, VMEM],
        out_specs=VMEM,
        compiler_params=params(32),
        name="pick",
    )(requests.reshape(rows, 1), features)
    buffer = lax.all_to_all(
        outgoing.reshape(peers, per_owner, channels), "wide", split_axis=0, concat_axis=0, tiled=True
    ).reshape(rows, channels)
    shape = jax.ShapeDtypeStruct
    grams = pl.pallas_call(
        gram_kernel,
        out_shape=(
            shape((rows, rows), bf16),
            shape((rows, rows), bf16),
            shape((rows, width), bf16),
            shape((rows, width), bf16),
            shape((rows, channels), f32),
            shape((channels, channels), bf16),
            shape((channels, channels), bf16),
            shape((8, lanes), f32),
        ),
        in_specs=[SMEM, VMEM, VMEM, VMEM, ANY, ANY],
        out_specs=(VMEM,) * 8,
        scratch_shapes=[
            pltpu.VMEM((tiles, list_len, pixels), jnp.int32),
            pltpu.VMEM((tiles * pixels, width), bf16),
            pltpu.VMEM((rows, slots), bf16),
            pltpu.VMEM((rows, slots), bf16),
            pltpu.VMEM((rows, slots), bf16),
            pltpu.VMEM((slots, pixels), bf16),
            pltpu.VMEM((slots, width), bf16),
            pltpu.VMEM((slots, width), bf16),
            pltpu.SemaphoreType.DMA((tiles // 2,)),
            pltpu.SemaphoreType.DMA((tiles,)),
        ],
        cost_estimate=pl.CostEstimate(
            flops=2 * slots * pixels * width + 4 * rows * slots * (width + rows),
            bytes_accessed=targets.size * 2 + alpha_codes.size * 4,
            transcendentals=2 * alpha_codes.size,
        ),
        compiler_params=params(48),
        name="gram",
    )(
        list_counts,
        tile_lists.reshape(tiles // 2, 2 * list_len),
        depth_order.reshape(tiles // 2, 2 * list_len),
        dec_weight,
        alpha_codes,
        targets,
    )
    half_shape = shape((chunks, body + per_owner + 8, lanes), f32)
    send, keep = pl.pallas_call(
        gradient_kernel,
        out_shape=(half_shape, half_shape),
        in_specs=[SMEM] + [VMEM] * 10,
        out_specs=(VMEM, VMEM),
        scratch_shapes=[pltpu.VMEM((rows, channels), f32)],
        compiler_params=params(48),
        name="gradient",
    )(parity.reshape(1), buffer, *grams, dec_weight)
    got = lax.ppermute(send, "wide", [(i, i ^ 1) for i in range(peers)])
    joined = pl.pallas_call(
        functools.partial(join_kernel, body, per_owner),
        out_shape=shape((chunks, body + 2 * per_owner + 8, lanes), f32),
        in_specs=[VMEM, VMEM],
        out_specs=VMEM,
        compiler_params=params(16),
        name="join",
    )(keep, got)
    returned = lax.all_to_all(
        joined,
        "wide",
        split_axis=0,
        concat_axis=0,
        axis_index_groups=[[2 * i + c for i in range(chunks)] for c in range(2)],
        tiled=True,
    )
    sides = requests.reshape(chunks, 2, per_owner)
    sides = jnp.where(parity == 0, sides, sides[:, ::-1]).reshape(1, rows)
    pixel_total = peers * tiles * pixels
    feat_grad, dec_grad, loss = pl.pallas_call(
        functools.partial(
            finish_kernel,
            body,
            per_owner,
            1.0 / math.sqrt(pixel_total),
            0.5 / (pixel_total * width),
        ),
        out_shape=(
            shape((owned, channels), f32),
            shape((share, width), f32),
            shape((1, lanes), f32),
        ),
        in_specs=[VMEM, VMEM],
        out_specs=(VMEM,) * 3,
        compiler_params=params(32),
        name="finish",
    )(sides, returned)
    return (feat_grad, dec_grad, loss[0, :1])


def solution(mesh):
    return jax.shard_map(
        local,
        mesh=mesh,
        in_specs=(
            P(("groups", "wide"), None),
            P("groups", "wide", None),
            P(("groups", "wide"), None),
            P(("groups", "wide"), None),
            P(("groups", "wide"), None, None),
            P(("groups", "wide"), None),
            P(("groups", "wide"), None),
            P(),
        ),
        out_specs=(P(("groups", "wide"), None), P(("groups", "wide"), None), P("groups")),
        check_vma=False,
    )
```

```python
import functools
import math

import jax
import jax.numpy as jnp
from jax import lax
from jax.experimental import pallas as pl
from jax.experimental.pallas import tpu as pltpu
from jax.sharding import PartitionSpec as P

ALPHA_TOP = 0.1
NN = (((1,), (0,)), ((), ()))
NT = (((1,), (1,)), ((), ()))
TN = (((0,), (0,)), ((), ()))
VMEM = pl.BlockSpec(memory_space=pltpu.VMEM)
SMEM = pl.BlockSpec(memory_space=pltpu.SMEM)
ANY = pl.BlockSpec(memory_space=pl.ANY)
HBM = pl.BlockSpec(memory_space=pltpu.HBM)
CODE_TOP = 32000.0
LOSS_TOP = 16384.0
META = 16


def dot(a, b, dims=NN):
    return lax.dot_general(a, b, dims, preferred_element_type=jnp.float32)


def split(x):
    high = x.astype(jnp.bfloat16)
    return high, (x - high.astype(jnp.float32)).astype(jnp.bfloat16)


def one_hot(condition):
    return jnp.where(condition, 1.0, 0.0).astype(jnp.bfloat16)


def pin(x):
    return pltpu.with_memory_space_constraint(x, pltpu.HBM)


def params(mib):
    return pltpu.CompilerParams(vmem_limit_bytes=mib << 20)


def pick_kernel(request_ref, feature_hbm, out_ref, held, sem):
    copy = pltpu.make_async_copy(feature_hbm, held, sem)
    copy.start()
    peers, _, per_owner = request_ref.shape
    owned = held.shape[0]
    lane = lax.broadcasted_iota(jnp.int32, (peers, per_owner, owned), 2)
    wanted = request_ref[...][:, 0, :]
    chosen = jnp.where(wanted[:, :, None] == lane, 1.0, 0.0)
    chosen = chosen.reshape(peers * per_owner, owned).astype(jnp.bfloat16)
    copy.wait()
    out_ref[...] = dot(chosen, held[...]).astype(jnp.bfloat16)


def gram_kernel(
    count_hbm,
    list_hbm,
    order_hbm,
    weight_hbm,
    code_hbm,
    target_hbm,
    gram_high_ref,
    gram_low_ref,
    cross_high_ref,
    cross_low_ref,
    back_ref,
    square_high_ref,
    square_low_ref,
    loss_ref,
    counts,
    lists,
    orders,
    weights,
    codes,
    target,
    hot,
    blends,
    bt_high,
    bt_low,
    cross,
    first_sem,
    target_sem,
):
    tiles, list_len, pixels = codes.shape
    rows = gram_high_ref.shape[0]
    both = 2 * list_len
    pairs = tiles // 2
    small = [
        pltpu.make_async_copy(source, goal, first_sem.at[i])
        for i, (source, goal) in enumerate(
            (
                (count_hbm, counts),
                (list_hbm, lists),
                (order_hbm, orders),
                (code_hbm, codes),
                (weight_hbm, weights),
            )
        )
    ]
    walk = [i + side * pairs for i in range(pairs) for side in range(2)]
    target_copies = {
        t: pltpu.make_async_copy(
            target_hbm.at[pl.ds(t * pixels, pixels)],
            target.at[pl.ds(t * pixels, pixels)],
            target_sem.at[t],
        )
        for t in walk
    }
    for copy in small:
        copy.start()
    for t in walk:
        target_copies[t].start()
    row = lax.broadcasted_iota(jnp.int32, (both, both), 0)
    lane = lax.broadcasted_iota(jnp.int32, (both, both), 1)
    same = (row >= list_len) == (lane >= list_len)
    steps = lane.astype(jnp.float32)
    slot = lax.broadcasted_iota(jnp.int32, (both, 1), 0)
    place = lax.broadcasted_iota(jnp.int32, (rows, both), 0)
    for copy in small:
        copy.wait()
    order = jnp.concatenate([orders[:pairs, :], orders[pairs:, :] + list_len], axis=1)
    listed = jnp.concatenate([lists[:pairs, :], lists[pairs:, :]], axis=1)
    weight = weights[...]
    high, low = split(dot(weight, weight, NT))
    square_high_ref[...] = high
    square_low_ref[...] = low
    ranks, nearer = [], []
    for i in range(pairs):
        at = row == order[i : i + 1, :]
        rank = jnp.sum(jnp.where(at, steps, 0.0), axis=1, keepdims=True)
        ahead = same & (steps < rank)
        ranks.append(rank)
        nearer.append(dot(one_hot(ahead), one_hot(at), NT).astype(jnp.bfloat16))
    values = []
    for i in range(pairs):
        code = jnp.concatenate([codes[i], codes[i + pairs]], axis=0)
        alpha = code.astype(jnp.float32) * (ALPHA_TOP / 255.0)
        high, low = split(jnp.log(1.0 - alpha))
        transmit = jnp.exp(dot(nearer[i], high) + dot(nearer[i], low))
        limit = jnp.where(slot < list_len, counts[0, i], counts[0, i + pairs] + list_len)
        live = ranks[i] < limit.astype(jnp.float32)
        blend = jnp.where(live, transmit * alpha, 0.0).astype(jnp.bfloat16)
        blends[i * both : (i + 1) * both, :] = blend
        values.append(blend)
    inner = [split(jnp.where(same, dot(v, v, NT), 0.0)) for v in values]
    gram = jnp.zeros((rows, rows), jnp.float32)
    for i in range(pairs):
        chosen = one_hot(listed[i : i + 1, :] == place)
        hot[:, i * both : (i + 1) * both] = chosen
        high, low = split(dot(chosen, inner[i][0]) + dot(chosen, inner[i][1]))
        gram = gram + (dot(high, chosen, NT) + dot(low, chosen, NT))
    high, low = split(gram)
    gram_high_ref[...] = high
    gram_low_ref[...] = low
    total = jnp.zeros((8, target.shape[1]), jnp.float32)
    group = 2
    for i in range(pairs):
        for side in range(2):
            t = i + side * pairs
            target_copies[t].wait()
            goal = target[t * pixels : (t + 1) * pixels, :]
            begin = i * both + side * list_len
            own = slice(begin, begin + list_len)
            high, low = split(dot(blends[own, :], goal))
            bt_high[own, :] = high
            bt_low[own, :] = low
            wide = goal.astype(jnp.float32)
            total = total + jnp.sum((wide * wide).reshape(pixels // 8, 8, -1), axis=0)
        if i % group == group - 1:
            own = slice((i + 1 - group) * both, (i + 1) * both)
            chosen = hot[:, own]
            more = dot(chosen, bt_high[own, :]) + dot(chosen, bt_low[own, :])
            if i >= group:
                more = cross[...] + more
            if i < pairs - 1:
                cross[...] = more
    loss_ref[...] = jnp.full(loss_ref.shape, jnp.sum(total), jnp.float32)
    high, low = split(more)
    cross_high_ref[...] = high
    cross_low_ref[...] = low
    back_ref[...] = dot(high, weight, NT) + dot(low, weight, NT)


def gradient_kernel(
    parity_ref,
    buffer_ref,
    gram_high_ref,
    gram_low_ref,
    cross_high_ref,
    cross_low_ref,
    back_ref,
    square_high_ref,
    square_low_ref,
    loss_ref,
    weight_ref,
    send_ref,
    keep_ref,
    grads,
):
    parity = parity_ref[0]
    buffer = buffer_ref[...]
    rows, channels = buffer.shape
    chunks = send_ref.shape[0]
    per_owner = rows // (2 * chunks)
    share = channels // (2 * chunks)
    lanes = 128
    width = weight_ref.shape[1]
    strips = width // lanes
    body = share * strips
    half = channels // 2
    mixed = dot(gram_high_ref[...], buffer) + dot(gram_low_ref[...], buffer)
    high, low = split(mixed)
    square_high = square_high_ref[...]
    back = back_ref[...]
    slope = dot(high, square_high) + dot(low, square_high) + dot(high, square_low_ref[...]) - back
    grads[...] = slope
    loss = loss_ref[...] + jnp.sum(buffer.astype(jnp.float32) * (slope - back))
    source = lax.broadcasted_iota(jnp.int32, (channels, channels), 0)
    goal = lax.broadcasted_iota(jnp.int32, (channels, channels), 1)
    second = goal >= half
    inner = jnp.where(second, goal - half, goal)
    side = jnp.where(second, parity, 1 - parity)
    chunk = inner // share
    wanted = chunk * (2 * share) + side * share + (inner - chunk * share)
    ordered = dot(buffer, one_hot(source == wanted)).astype(jnp.bfloat16)
    core_high, core_low = split(dot(ordered, high, TN) + dot(ordered, low, TN))
    weight = weight_ref[...]
    grad = dot(core_high, weight) + dot(core_low, weight)
    grad = grad - dot(ordered, cross_high_ref[...], TN) - dot(ordered, cross_low_ref[...], TN)
    for number, (ref, which) in enumerate(((send_ref, 1 - parity), (keep_ref, parity))):
        for i in range(chunks):
            top = number * half + i * share
            for j in range(strips):
                ref[i, j * share : (j + 1) * share, :] = grad[
                    top : top + share, j * lanes : (j + 1) * lanes
                ]
            begin = pl.multiple_of((2 * i + which) * per_owner, per_owner)
            ref[i, body : body + per_owner, :] = grads[pl.ds(begin, per_owner), :]
            ref[i, body + per_owner :, :] = loss


def scale_bits(x):
    top = jnp.max(jnp.abs(x), axis=-2, keepdims=True)
    return jnp.ceil(jnp.log2(jnp.maximum(top, 1e-30)))


def to_code(x):
    return jnp.round(x).astype(jnp.int32).astype(jnp.int16)


def from_code(x):
    return x.astype(jnp.int32).astype(jnp.float32)


def join_kernel(body, per_owner, keep_ref, got_ref, out_ref):
    chunks, _, lanes = keep_ref.shape
    ends = body + 2 * per_owner
    dec = keep_ref[:, :body, :] + got_ref[:, :body, :]
    dec_bits = scale_bits(dec)
    out_ref[:, :body, :] = to_code(dec * (CODE_TOP * jnp.exp2(-dec_bits)))
    rows = slice(body, body + per_owner)
    moved = jnp.concatenate([keep_ref[:, rows, :], got_ref[:, rows, :]], axis=1)
    bits = scale_bits(moved)
    out_ref[:, body:ends, :] = to_code(moved * (CODE_TOP * jnp.exp2(-bits)))
    loss = keep_ref[:, body + per_owner :, :] + got_ref[:, body + per_owner :, :]
    loss = loss[:, :1, :]
    loss_bits = scale_bits(loss)
    loss = loss * (LOSS_TOP * jnp.exp2(-loss_bits))
    high = jnp.round(loss)
    low = (loss - high) * LOSS_TOP
    at = lax.broadcasted_iota(jnp.int32, (chunks, META, lanes), 1)
    meta = jnp.zeros((chunks, META, lanes), jnp.float32)
    for i, value in enumerate((dec_bits, bits, loss_bits, high, low)):
        meta = jnp.where(at == i, value, meta)
    out_ref[:, ends:, :] = to_code(meta)


def place_kernel(parity_ref, request_ref, after_ref, out_ref):
    del after_ref
    peers = request_ref.shape[0]
    rows = request_ref[...][:, 0, :]
    even = jnp.concatenate([rows[d : d + 1, :] for d in range(peers)], axis=1)
    odd = jnp.concatenate([rows[d ^ 1 : (d ^ 1) + 1, :] for d in range(peers)], axis=1)
    wanted = jnp.where(parity_ref[0] == 0, even, odd)
    out_ref[...] = one_hot(lax.broadcasted_iota(jnp.int32, out_ref.shape, 0) == wanted)


def finish_kernel(
    body, per_owner, dec_scale, loss_scale, chosen_ref, got_ref, feat_ref, dec_ref, loss_ref
):
    chunks, _, lanes = got_ref.shape
    share = dec_ref.shape[0]
    ends = body + 2 * per_owner
    meta = from_code(got_ref[:, ends:, :])
    dec = from_code(got_ref[:, :body, :]) * jnp.exp2(meta[:, 0:1, :])
    total = jnp.sum(dec, axis=0) * (dec_scale / CODE_TOP)
    for j in range(body // share):
        dec_ref[:, j * lanes : (j + 1) * lanes] = total[j * share : (j + 1) * share, :]
    loss = (meta[:, 3:4, :] + meta[:, 4:5, :] * (1.0 / LOSS_TOP)) * jnp.exp2(meta[:, 2:3, :])
    loss_ref[...] = jnp.sum(loss, axis=0) * (loss_scale / LOSS_TOP)
    moved = from_code(got_ref[:, body:ends, :]) * (jnp.exp2(meta[:, 1:2, :]) / CODE_TOP)
    high, low = split(moved.reshape(chunks * 2 * per_owner, lanes))
    chosen = chosen_ref[...]
    feat_ref[...] = dot(chosen, high) + dot(chosen, low)


def local(
    features, fetch_ids, tile_lists, depth_order, alpha_codes, list_counts, targets, dec_weight
):
    f32, bf16 = jnp.float32, jnp.bfloat16
    peers = lax.axis_size("wide")
    owned, channels = features.shape
    per_owner = fetch_ids.shape[2]
    rows = peers * per_owner
    tiles, list_len, pixels = alpha_codes.shape
    width = targets.shape[1]
    slots = tiles * list_len
    chunks = peers // 2
    share = channels // peers
    lanes = 128
    body = share * (width // lanes)
    parity = lax.rem(lax.axis_index("wide"), 2)
    shape = jax.ShapeDtypeStruct
    outgoing = pl.pallas_call(
        pick_kernel,
        out_shape=shape((rows, channels), bf16),
        in_specs=[VMEM, HBM],
        out_specs=VMEM,
        scratch_shapes=[pltpu.VMEM((owned, channels), bf16), pltpu.SemaphoreType.DMA],
        compiler_params=params(32),
        name="pick",
    )(pin(fetch_ids), pin(features))
    buffer = lax.all_to_all(
        outgoing.reshape(peers, per_owner, channels), "wide", split_axis=0, concat_axis=0, tiled=True
    ).reshape(rows, channels)
    grams = pl.pallas_call(
        gram_kernel,
        out_shape=(
            shape((rows, rows), bf16),
            shape((rows, rows), bf16),
            shape((rows, width), bf16),
            shape((rows, width), bf16),
            shape((rows, channels), f32),
            shape((channels, channels), bf16),
            shape((channels, channels), bf16),
            shape((8, lanes), f32),
        ),
        in_specs=[HBM] * 6,
        out_specs=(VMEM,) * 8,
        scratch_shapes=[
            pltpu.SMEM((1, tiles), jnp.int32),
            pltpu.VMEM((tiles, list_len), jnp.int32),
            pltpu.VMEM((tiles, list_len), jnp.int32),
            pltpu.VMEM((channels, width), bf16),
            pltpu.VMEM((tiles, list_len, pixels), jnp.int32),
            pltpu.VMEM((tiles * pixels, width), bf16),
            pltpu.VMEM((rows, slots), bf16),
            pltpu.VMEM((slots, pixels), bf16),
            pltpu.VMEM((slots, width), bf16),
            pltpu.VMEM((slots, width), bf16),
            pltpu.VMEM((rows, width), f32),
            pltpu.SemaphoreType.DMA((5,)),
            pltpu.SemaphoreType.DMA((tiles,)),
        ],
        cost_estimate=pl.CostEstimate(
            flops=2 * slots * pixels * width + 4 * rows * slots * (width + rows),
            bytes_accessed=targets.size * 2 + alpha_codes.size * 4,
            transcendentals=2 * alpha_codes.size,
        ),
        compiler_params=params(44),
        name="gram",
    )(*map(pin, (list_counts, tile_lists, depth_order, dec_weight, alpha_codes, targets)))
    half_shape = shape((chunks, body + per_owner + 8, lanes), f32)
    send, keep = pl.pallas_call(
        gradient_kernel,
        out_shape=(half_shape, half_shape),
        in_specs=[SMEM] + [VMEM] * 10,
        out_specs=(VMEM, VMEM),
        scratch_shapes=[pltpu.VMEM((rows, channels), f32)],
        compiler_params=params(40),
        name="gradient",
    )(parity.reshape(1), buffer, *grams, dec_weight)
    got = lax.ppermute(send, "wide", [(i, i ^ 1) for i in range(peers)])
    joined = pl.pallas_call(
        functools.partial(join_kernel, body, per_owner),
        out_shape=shape((chunks, body + 2 * per_owner + META, lanes), jnp.int16),
        in_specs=[VMEM, VMEM],
        out_specs=VMEM,
        compiler_params=params(32),
        name="join",
    )(keep, got)
    returned = lax.all_to_all(
        joined,
        "wide",
        split_axis=0,
        concat_axis=0,
        axis_index_groups=[[2 * i + c for i in range(chunks)] for c in range(2)],
        tiled=True,
    )
    chosen = pl.pallas_call(
        place_kernel,
        out_shape=shape((owned, rows), bf16),
        in_specs=[SMEM, VMEM, ANY],
        out_specs=VMEM,
        compiler_params=params(32),
        name="place",
    )(parity.reshape(1), fetch_ids, joined)
    pixel_total = peers * tiles * pixels
    feat_grad, dec_grad, loss = pl.pallas_call(
        functools.partial(
            finish_kernel,
            body,
            per_owner,
            1.0 / math.sqrt(pixel_total),
            0.5 / (pixel_total * width),
        ),
        out_shape=(
            shape((owned, channels), f32),
            shape((share, width), f32),
            shape((1, lanes), f32),
        ),
        in_specs=[VMEM, VMEM],
        out_specs=(VMEM,) * 3,
        compiler_params=params(32),
        name="finish",
    )(chosen, returned)
    return (feat_grad, dec_grad, loss[0, :1])


def solution(mesh):
    return jax.shard_map(
        local,
        mesh=mesh,
        in_specs=(
            P(("groups", "wide"), None),
            P("groups", "wide", None),
            P(("groups", "wide"), None),
            P(("groups", "wide"), None),
            P(("groups", "wide"), None, None),
            P(("groups", "wide"), None),
            P(("groups", "wide"), None),
            P(),
        ),
        out_specs=(P(("groups", "wide"), None), P(("groups", "wide"), None), P("groups")),
        check_vma=False,
    )
```

```python
import functools
import math

import jax
import jax.numpy as jnp
from jax import lax
from jax.experimental import pallas as pl
from jax.experimental.pallas import tpu as pltpu
from jax.sharding import PartitionSpec as P

ALPHA_TOP = 0.1
NN = (((1,), (0,)), ((), ()))
NT = (((1,), (1,)), ((), ()))
TN = (((0,), (0,)), ((), ()))
VMEM = pl.BlockSpec(memory_space=pltpu.VMEM)
SMEM = pl.BlockSpec(memory_space=pltpu.SMEM)
ANY = pl.BlockSpec(memory_space=pl.ANY)
HBM = pl.BlockSpec(memory_space=pltpu.HBM)
CODE_TOP = 32000.0
LOSS_TOP = 16384.0
META = 16


def dot(a, b, dims=NN):
    return lax.dot_general(a, b, dims, preferred_element_type=jnp.float32)


def split(x):
    high = x.astype(jnp.bfloat16)
    return high, (x - high.astype(jnp.float32)).astype(jnp.bfloat16)


def one_hot(condition):
    return jnp.where(condition, 1.0, 0.0).astype(jnp.bfloat16)


def pin(x):
    return pltpu.with_memory_space_constraint(x, pltpu.HBM)


def near(x):
    return pltpu.with_memory_space_constraint(x, pltpu.VMEM)


def params(mib):
    return pltpu.CompilerParams(vmem_limit_bytes=mib << 20)


def pick_kernel(request_hbm, feature_hbm, out_ref, wanted, held, sems):
    copies = [
        pltpu.make_async_copy(request_hbm, wanted, sems.at[0]),
        pltpu.make_async_copy(feature_hbm, held, sems.at[1]),
    ]
    for copy in copies:
        copy.start()
    peers, _, per_owner = wanted.shape
    owned = held.shape[0]
    lane = lax.broadcasted_iota(jnp.int32, (peers, per_owner, owned), 2)
    copies[0].wait()
    chosen = jnp.where(wanted[...][:, 0, :][:, :, None] == lane, 1.0, 0.0)
    chosen = chosen.reshape(peers * per_owner, owned).astype(jnp.bfloat16)
    copies[1].wait()
    out_ref[...] = dot(chosen, held[...]).astype(jnp.bfloat16)


def gram_kernel(
    count_ref,
    list_ref,
    order_ref,
    weight_ref,
    code_ref,
    target_hbm,
    gram_high_ref,
    gram_low_ref,
    cross_high_ref,
    cross_low_ref,
    back_ref,
    square_high_ref,
    square_low_ref,
    loss_ref,
    hot,
    part_high,
    part_low,
    blends,
    bt_high,
    bt_low,
    target,
    cross,
    sems,
):
    tiles, list_len, pixels = code_ref.shape
    rows = gram_high_ref.shape[0]
    both = 2 * list_len
    pairs = tiles // 2
    part = pairs // 2
    copies = []
    for i, first in enumerate((0, pairs, part, pairs + part)):
        span = pl.ds(first * pixels, part * pixels)
        copies.append(pltpu.make_async_copy(target_hbm.at[span], target.at[span], sems.at[i]))
    for copy in copies:
        copy.start()
    row = lax.broadcasted_iota(jnp.int32, (both, both), 0)
    lane = lax.broadcasted_iota(jnp.int32, (both, both), 1)
    same = (row >= list_len) == (lane >= list_len)
    steps = lane.astype(jnp.float32)
    slot = lax.broadcasted_iota(jnp.int32, (both, 1), 0)
    place = lax.broadcasted_iota(jnp.int32, (rows, both), 0)
    order = jnp.concatenate([order_ref[:pairs, :], order_ref[pairs:, :] + list_len], axis=1)
    listed = jnp.concatenate([list_ref[:pairs, :], list_ref[pairs:, :]], axis=1)
    weight = weight_ref[...]
    high, low = split(dot(weight, weight, NT))
    square_high_ref[...] = high
    square_low_ref[...] = low
    ranks, nearer = [], []
    for i in range(pairs):
        at = row == order[i : i + 1, :]
        rank = jnp.sum(jnp.where(at, steps, 0.0), axis=1, keepdims=True)
        ahead = same & (steps < rank)
        ranks.append(rank)
        nearer.append(dot(one_hot(ahead), one_hot(at), NT).astype(jnp.bfloat16))
    values = []
    for i in range(pairs):
        code = jnp.concatenate([code_ref[i], code_ref[i + pairs]], axis=0)
        alpha = code.astype(jnp.float32) * (ALPHA_TOP / 255.0)
        logs = jnp.concatenate(split(jnp.log(1.0 - alpha)), axis=0)
        transmit = jnp.exp(dot(jnp.concatenate([nearer[i]] * 2, axis=1), logs))
        first = count_ref[:, i : i + 1]
        second = count_ref[:, i + pairs : i + pairs + 1] + list_len
        limit = jnp.where(slot < list_len, first, second)
        live = ranks[i] < limit.astype(jnp.float32)
        blend = jnp.where(live, transmit * alpha, 0.0).astype(jnp.bfloat16)
        blends[i * both : (i + 1) * both, :] = blend
        values.append(blend)
    inner = [split(jnp.where(same, dot(v, v, NT), 0.0)) for v in values]
    for i in range(pairs):
        own = slice(i * both, (i + 1) * both)
        chosen = one_hot(listed[i : i + 1, :] == place)
        hot[:, own] = chosen
        wide = dot(chosen, jnp.concatenate(inner[i], axis=1))
        high, low = split(wide[:, :both] + wide[:, both:])
        part_high[:, own] = high
        part_low[:, own] = low
    chosen = hot[...]
    high, low = split(dot(part_high[...], chosen, NT) + dot(part_low[...], chosen, NT))
    gram_high_ref[...] = high
    gram_low_ref[...] = low
    total = jnp.zeros((8, target.shape[1]), jnp.float32)
    for half in range(2):
        copies[2 * half].wait()
        copies[2 * half + 1].wait()
        for i in range(half * part, (half + 1) * part):
            for side in range(2):
                t = i + side * pairs
                goal = target[t * pixels : (t + 1) * pixels, :]
                begin = i * both + side * list_len
                own = slice(begin, begin + list_len)
                high, low = split(dot(blends[own, :], goal))
                bt_high[own, :] = high
                bt_low[own, :] = low
                wide = goal.astype(jnp.float32)
                total = total + jnp.sum((wide * wide).reshape(pixels // 8, 8, -1), axis=0)
        own = slice(half * part * both, (half + 1) * part * both)
        chosen = hot[:, own]
        more = dot(chosen, bt_high[own, :]) + dot(chosen, bt_low[own, :])
        if half == 0:
            cross[...] = more
    loss_ref[...] = jnp.full(loss_ref.shape, jnp.sum(total), jnp.float32)
    high, low = split(cross[...] + more)
    cross_high_ref[...] = high
    cross_low_ref[...] = low
    back_ref[...] = dot(high, weight, NT) + dot(low, weight, NT)


def gradient_kernel(
    parity_ref,
    buffer_ref,
    gram_high_ref,
    gram_low_ref,
    cross_high_ref,
    cross_low_ref,
    back_ref,
    square_high_ref,
    square_low_ref,
    loss_ref,
    weight_ref,
    send_ref,
    keep_ref,
    grads,
):
    parity = parity_ref[0]
    buffer = buffer_ref[...]
    rows, channels = buffer.shape
    chunks = send_ref.shape[0]
    per_owner = rows // (2 * chunks)
    share = channels // (2 * chunks)
    lanes = 128
    width = weight_ref.shape[1]
    strips = width // lanes
    body = share * strips
    half = channels // 2
    mixed = dot(gram_high_ref[...], buffer) + dot(gram_low_ref[...], buffer)
    high, low = split(mixed)
    square_high = square_high_ref[...]
    back = back_ref[...]
    slope = dot(high, square_high) + dot(low, square_high) + dot(high, square_low_ref[...]) - back
    grads[...] = slope
    loss = loss_ref[...] + jnp.sum(buffer.astype(jnp.float32) * (slope - back))
    source = lax.broadcasted_iota(jnp.int32, (channels, channels), 0)
    goal = lax.broadcasted_iota(jnp.int32, (channels, channels), 1)
    second = goal >= half
    inner = jnp.where(second, goal - half, goal)
    side = jnp.where(second, parity, 1 - parity)
    chunk = inner // share
    wanted = chunk * (2 * share) + side * share + (inner - chunk * share)
    ordered = dot(buffer, one_hot(source == wanted)).astype(jnp.bfloat16)
    core_high, core_low = split(dot(ordered, high, TN) + dot(ordered, low, TN))
    weight = weight_ref[...]
    grad = dot(core_high, weight) + dot(core_low, weight)
    grad = grad - dot(ordered, cross_high_ref[...], TN) - dot(ordered, cross_low_ref[...], TN)
    for number, (ref, which) in enumerate(((send_ref, 1 - parity), (keep_ref, parity))):
        for i in range(chunks):
            top = number * half + i * share
            for j in range(strips):
                ref[i, j * share : (j + 1) * share, :] = grad[
                    top : top + share, j * lanes : (j + 1) * lanes
                ]
            begin = pl.multiple_of((2 * i + which) * per_owner, per_owner)
            ref[i, body : body + per_owner, :] = grads[pl.ds(begin, per_owner), :]
            ref[i, body + per_owner :, :] = loss


def scale_bits(x):
    top = jnp.max(jnp.abs(x), axis=-2, keepdims=True)
    return jnp.ceil(jnp.log2(jnp.maximum(top, 1e-30)))


def to_code(x):
    return jnp.round(x).astype(jnp.int32).astype(jnp.int16)


def from_code(x):
    return x.astype(jnp.int32).astype(jnp.float32)


def join_kernel(body, per_owner, keep_ref, got_ref, out_ref):
    chunks, _, lanes = keep_ref.shape
    ends = body + 2 * per_owner
    dec = keep_ref[:, :body, :] + got_ref[:, :body, :]
    dec_bits = scale_bits(dec)
    out_ref[:, :body, :] = to_code(dec * (CODE_TOP * jnp.exp2(-dec_bits)))
    rows = slice(body, body + per_owner)
    moved = jnp.concatenate([keep_ref[:, rows, :], got_ref[:, rows, :]], axis=1)
    bits = scale_bits(moved)
    out_ref[:, body:ends, :] = to_code(moved * (CODE_TOP * jnp.exp2(-bits)))
    loss = keep_ref[:, body + per_owner :, :] + got_ref[:, body + per_owner :, :]
    loss = loss[:, :1, :]
    loss_bits = scale_bits(loss)
    loss = loss * (LOSS_TOP * jnp.exp2(-loss_bits))
    high = jnp.round(loss)
    low = (loss - high) * LOSS_TOP
    at = lax.broadcasted_iota(jnp.int32, (chunks, META, lanes), 1)
    meta = jnp.zeros((chunks, META, lanes), jnp.float32)
    for i, value in enumerate((dec_bits, bits, loss_bits, high, low)):
        meta = jnp.where(at == i, value, meta)
    out_ref[:, ends:, :] = to_code(meta)


def place_kernel(parity_ref, request_ref, after_ref, out_ref):
    del after_ref
    peers = request_ref.shape[0]
    rows = request_ref[...][:, 0, :]
    even = jnp.concatenate([rows[d : d + 1, :] for d in range(peers)], axis=1)
    odd = jnp.concatenate([rows[d ^ 1 : (d ^ 1) + 1, :] for d in range(peers)], axis=1)
    wanted = jnp.where(parity_ref[0] == 0, even, odd)
    out_ref[...] = one_hot(lax.broadcasted_iota(jnp.int32, out_ref.shape, 0) == wanted)


def finish_kernel(
    body, per_owner, dec_scale, loss_scale, chosen_ref, got_ref, feat_ref, dec_ref, loss_ref
):
    chunks, _, lanes = got_ref.shape
    share = dec_ref.shape[0]
    ends = body + 2 * per_owner
    meta = from_code(got_ref[:, ends:, :])
    dec = from_code(got_ref[:, :body, :]) * jnp.exp2(meta[:, 0:1, :])
    total = jnp.sum(dec, axis=0) * (dec_scale / CODE_TOP)
    for j in range(body // share):
        dec_ref[:, j * lanes : (j + 1) * lanes] = total[j * share : (j + 1) * share, :]
    loss = (meta[:, 3:4, :] + meta[:, 4:5, :] * (1.0 / LOSS_TOP)) * jnp.exp2(meta[:, 2:3, :])
    loss_ref[...] = jnp.sum(loss, axis=0) * (loss_scale / LOSS_TOP)
    moved = from_code(got_ref[:, body:ends, :]) * (jnp.exp2(meta[:, 1:2, :]) / CODE_TOP)
    high, low = split(moved.reshape(chunks * 2 * per_owner, lanes))
    chosen = chosen_ref[...]
    feat_ref[...] = dot(chosen, high) + dot(chosen, low)


def local(
    features, fetch_ids, tile_lists, depth_order, alpha_codes, list_counts, targets, dec_weight
):
    f32, bf16 = jnp.float32, jnp.bfloat16
    peers = lax.axis_size("wide")
    owned, channels = features.shape
    per_owner = fetch_ids.shape[2]
    rows = peers * per_owner
    tiles, list_len, pixels = alpha_codes.shape
    width = targets.shape[1]
    slots = tiles * list_len
    chunks = peers // 2
    share = channels // peers
    lanes = 128
    body = share * (width // lanes)
    parity = lax.rem(lax.axis_index("wide"), 2)
    shape = jax.ShapeDtypeStruct
    outgoing = pl.pallas_call(
        pick_kernel,
        out_shape=shape((rows, channels), bf16),
        in_specs=[HBM, HBM],
        out_specs=VMEM,
        scratch_shapes=[
            pltpu.VMEM((peers, 1, per_owner), jnp.int32),
            pltpu.VMEM((owned, channels), bf16),
            pltpu.SemaphoreType.DMA((2,)),
        ],
        cost_estimate=pl.CostEstimate(
            flops=20_000_000_000, bytes_accessed=40_000_000, transcendentals=0
        ),
        compiler_params=params(16),
        name="pick",
    )(pin(fetch_ids), pin(features))
    buffer = lax.all_to_all(
        outgoing.reshape(peers, per_owner, channels), "wide", split_axis=0, concat_axis=0, tiled=True
    ).reshape(rows, channels)
    grams = pl.pallas_call(
        gram_kernel,
        out_shape=(
            shape((rows, rows), bf16),
            shape((rows, rows), bf16),
            shape((rows, width), bf16),
            shape((rows, width), bf16),
            shape((rows, channels), f32),
            shape((channels, channels), bf16),
            shape((channels, channels), bf16),
            shape((8, lanes), f32),
        ),
        in_specs=[VMEM] * 5 + [HBM],
        out_specs=(VMEM,) * 8,
        scratch_shapes=[
            pltpu.VMEM((rows, slots), bf16),
            pltpu.VMEM((rows, slots), bf16),
            pltpu.VMEM((rows, slots), bf16),
            pltpu.VMEM((slots, pixels), bf16),
            pltpu.VMEM((slots, width), bf16),
            pltpu.VMEM((slots, width), bf16),
            pltpu.VMEM((tiles * pixels, width), bf16),
            pltpu.VMEM((rows, width), f32),
            pltpu.SemaphoreType.DMA((4,)),
        ],
        cost_estimate=pl.CostEstimate(
            flops=2 * slots * pixels * width + 4 * rows * slots * (width + rows),
            bytes_accessed=targets.size * 2 + alpha_codes.size * 4,
            transcendentals=2 * alpha_codes.size,
        ),
        compiler_params=params(36),
        name="gram",
    )(*map(near, (list_counts, tile_lists, depth_order, dec_weight, alpha_codes)), pin(targets))
    half_shape = shape((chunks, body + per_owner + 8, lanes), f32)
    send, keep = pl.pallas_call(
        gradient_kernel,
        out_shape=(half_shape, half_shape),
        in_specs=[SMEM] + [VMEM] * 10,
        out_specs=(VMEM, VMEM),
        scratch_shapes=[pltpu.VMEM((rows, channels), f32)],
        compiler_params=params(24),
        name="gradient",
    )(parity.reshape(1), buffer, *grams, dec_weight)
    got = lax.ppermute(send, "wide", [(i, i ^ 1) for i in range(peers)])
    joined = pl.pallas_call(
        functools.partial(join_kernel, body, per_owner),
        out_shape=shape((chunks, body + 2 * per_owner + META, lanes), jnp.int16),
        in_specs=[VMEM, VMEM],
        out_specs=VMEM,
        compiler_params=params(32),
        name="join",
    )(keep, got)
    returned = lax.all_to_all(
        joined,
        "wide",
        split_axis=0,
        concat_axis=0,
        axis_index_groups=[[2 * i + c for i in range(chunks)] for c in range(2)],
        tiled=True,
    )
    chosen = pl.pallas_call(
        place_kernel,
        out_shape=shape((owned, rows), bf16),
        in_specs=[SMEM, VMEM, ANY],
        out_specs=VMEM,
        compiler_params=params(32),
        name="place",
    )(parity.reshape(1), fetch_ids, joined)
    pixel_total = peers * tiles * pixels
    feat_grad, dec_grad, loss = pl.pallas_call(
        functools.partial(
            finish_kernel,
            body,
            per_owner,
            1.0 / math.sqrt(pixel_total),
            0.5 / (pixel_total * width),
        ),
        out_shape=(
            shape((owned, channels), f32),
            shape((share, width), f32),
            shape((1, lanes), f32),
        ),
        in_specs=[VMEM, VMEM],
        out_specs=(VMEM,) * 3,
        compiler_params=params(32),
        name="finish",
    )(chosen, returned)
    return (feat_grad, dec_grad, loss[0, :1])


def solution(mesh):
    return jax.shard_map(
        local,
        mesh=mesh,
        in_specs=(
            P(("groups", "wide"), None),
            P("groups", "wide", None),
            P(("groups", "wide"), None),
            P(("groups", "wide"), None),
            P(("groups", "wide"), None, None),
            P(("groups", "wide"), None),
            P(("groups", "wide"), None),
            P(),
        ),
        out_specs=(P(("groups", "wide"), None), P(("groups", "wide"), None), P("groups")),
        check_vma=False,
    )
```

```python
import functools
import math

import jax
import jax.numpy as jnp
from jax import lax
from jax.experimental import pallas as pl
from jax.experimental.pallas import tpu as pltpu
from jax.sharding import PartitionSpec as P

ALPHA_TOP = 0.1
NN = (((1,), (0,)), ((), ()))
NT = (((1,), (1,)), ((), ()))
TN = (((0,), (0,)), ((), ()))
VMEM = pl.BlockSpec(memory_space=pltpu.VMEM)
SMEM = pl.BlockSpec(memory_space=pltpu.SMEM)
ANY = pl.BlockSpec(memory_space=pl.ANY)
HBM = pl.BlockSpec(memory_space=pltpu.HBM)
CODE_TOP = 32000.0
LOSS_TOP = 16384.0
META = 16


def dot(a, b, dims=NN):
    return lax.dot_general(a, b, dims, preferred_element_type=jnp.float32)


def split(x):
    high = x.astype(jnp.bfloat16)
    return high, (x - high.astype(jnp.float32)).astype(jnp.bfloat16)


def one_hot(condition):
    return jnp.where(condition, 1.0, 0.0).astype(jnp.bfloat16)


def pin(x):
    return pltpu.with_memory_space_constraint(x, pltpu.HBM)


def near(x):
    return pltpu.with_memory_space_constraint(x, pltpu.VMEM)


def params(mib):
    return pltpu.CompilerParams(vmem_limit_bytes=mib << 20)


def pick_kernel(request_hbm, feature_hbm, out_ref, wanted, held, sems):
    copies = [
        pltpu.make_async_copy(request_hbm, wanted, sems.at[0]),
        pltpu.make_async_copy(feature_hbm, held, sems.at[1]),
    ]
    for copy in copies:
        copy.start()
    peers, _, per_owner = wanted.shape
    owned = held.shape[0]
    lane = lax.broadcasted_iota(jnp.int32, (peers, per_owner, owned), 2)
    copies[0].wait()
    chosen = jnp.where(wanted[...][:, 0, :][:, :, None] == lane, 1.0, 0.0)
    chosen = chosen.reshape(peers * per_owner, owned).astype(jnp.bfloat16)
    copies[1].wait()
    out_ref[...] = dot(chosen, held[...]).astype(jnp.bfloat16)


def gram_kernel(
    count_ref,
    list_ref,
    order_ref,
    weight_ref,
    code_ref,
    target_hbm,
    gram_high_ref,
    gram_low_ref,
    cross_high_ref,
    cross_low_ref,
    back_ref,
    square_high_ref,
    square_low_ref,
    loss_ref,
    hot,
    part_high,
    part_low,
    blends,
    bt_high,
    bt_low,
    target,
    cross,
    sems,
):
    tiles, list_len, pixels = code_ref.shape
    rows = gram_high_ref.shape[0]
    both = 2 * list_len
    pairs = tiles // 2
    part = pairs // 2
    copies = []
    for i, first in enumerate((0, pairs, part, pairs + part)):
        span = pl.ds(first * pixels, part * pixels)
        copies.append(pltpu.make_async_copy(target_hbm.at[span], target.at[span], sems.at[i]))
    for copy in copies:
        copy.start()
    row = lax.broadcasted_iota(jnp.int32, (both, both), 0)
    lane = lax.broadcasted_iota(jnp.int32, (both, both), 1)
    same = (row >= list_len) == (lane >= list_len)
    steps = lane.astype(jnp.float32)
    slot = lax.broadcasted_iota(jnp.int32, (both, 1), 0)
    place = lax.broadcasted_iota(jnp.int32, (rows, both), 0)
    order = jnp.concatenate([order_ref[:pairs, :], order_ref[pairs:, :] + list_len], axis=1)
    listed = jnp.concatenate([list_ref[:pairs, :], list_ref[pairs:, :]], axis=1)
    weight = weight_ref[...]
    high, low = split(dot(weight, weight, NT))
    square_high_ref[...] = high
    square_low_ref[...] = low
    ranks, nearer = [], []
    for i in range(pairs):
        at = row == order[i : i + 1, :]
        rank = jnp.sum(jnp.where(at, steps, 0.0), axis=1, keepdims=True)
        ahead = same & (steps < rank)
        ranks.append(rank)
        nearer.append(dot(one_hot(ahead), one_hot(at), NT).astype(jnp.bfloat16))
    values = []
    for i in range(pairs):
        code = jnp.concatenate([code_ref[i], code_ref[i + pairs]], axis=0)
        alpha = code.astype(jnp.float32) * (ALPHA_TOP / 255.0)
        logs = jnp.concatenate(split(jnp.log(1.0 - alpha)), axis=0)
        transmit = jnp.exp(dot(jnp.concatenate([nearer[i]] * 2, axis=1), logs))
        first = count_ref[:, i : i + 1]
        second = count_ref[:, i + pairs : i + pairs + 1] + list_len
        limit = jnp.where(slot < list_len, first, second)
        live = ranks[i] < limit.astype(jnp.float32)
        blend = jnp.where(live, transmit * alpha, 0.0).astype(jnp.bfloat16)
        blends[i * both : (i + 1) * both, :] = blend
        values.append(blend)
    inner = [split(jnp.where(same, dot(v, v, NT), 0.0)) for v in values]
    for i in range(pairs):
        own = slice(i * both, (i + 1) * both)
        chosen = one_hot(listed[i : i + 1, :] == place)
        hot[:, own] = chosen
        wide = dot(chosen, jnp.concatenate(inner[i], axis=1))
        high, low = split(wide[:, :both] + wide[:, both:])
        part_high[:, own] = high
        part_low[:, own] = low
    chosen = hot[...]
    high, low = split(dot(part_high[...], chosen, NT) + dot(part_low[...], chosen, NT))
    gram_high_ref[...] = high
    gram_low_ref[...] = low
    total = jnp.zeros((8, target.shape[1]), jnp.float32)
    for half in range(2):
        copies[2 * half].wait()
        copies[2 * half + 1].wait()
        for i in range(half * part, (half + 1) * part):
            for side in range(2):
                t = i + side * pairs
                goal = target[t * pixels : (t + 1) * pixels, :]
                begin = i * both + side * list_len
                own = slice(begin, begin + list_len)
                high, low = split(dot(blends[own, :], goal))
                bt_high[own, :] = high
                bt_low[own, :] = low
                wide = goal.astype(jnp.float32)
                total = total + jnp.sum((wide * wide).reshape(pixels // 8, 8, -1), axis=0)
        own = slice(half * part * both, (half + 1) * part * both)
        chosen = hot[:, own]
        more = dot(chosen, bt_high[own, :]) + dot(chosen, bt_low[own, :])
        if half == 0:
            cross[...] = more
    loss_ref[...] = jnp.full(loss_ref.shape, jnp.sum(total), jnp.float32)
    high, low = split(cross[...] + more)
    cross_high_ref[...] = high
    cross_low_ref[...] = low
    back_ref[...] = dot(high, weight, NT) + dot(low, weight, NT)


def gradient_kernel(
    parity_ref,
    buffer_ref,
    gram_high_ref,
    gram_low_ref,
    cross_high_ref,
    cross_low_ref,
    back_ref,
    square_high_ref,
    square_low_ref,
    loss_ref,
    weight_ref,
    send_ref,
    keep_ref,
    grads,
):
    parity = parity_ref[0]
    buffer = buffer_ref[...]
    rows, channels = buffer.shape
    chunks = send_ref.shape[0]
    per_owner = rows // (2 * chunks)
    share = channels // (2 * chunks)
    lanes = 128
    width = weight_ref.shape[1]
    strips = width // lanes
    body = share * strips
    half = channels // 2
    mixed = dot(gram_high_ref[...], buffer) + dot(gram_low_ref[...], buffer)
    high, low = split(mixed)
    square_high = square_high_ref[...]
    back = back_ref[...]
    slope = dot(high, square_high) + dot(low, square_high) + dot(high, square_low_ref[...]) - back
    grads[...] = slope
    loss = loss_ref[...] + jnp.sum(buffer.astype(jnp.float32) * (slope - back))
    source = lax.broadcasted_iota(jnp.int32, (channels, channels), 0)
    goal = lax.broadcasted_iota(jnp.int32, (channels, channels), 1)
    second = goal >= half
    inner = jnp.where(second, goal - half, goal)
    side = jnp.where(second, parity, 1 - parity)
    chunk = inner // share
    wanted = chunk * (2 * share) + side * share + (inner - chunk * share)
    ordered = dot(buffer, one_hot(source == wanted)).astype(jnp.bfloat16)
    core_high, core_low = split(dot(ordered, high, TN) + dot(ordered, low, TN))
    weight = weight_ref[...]
    grad = dot(core_high, weight) + dot(core_low, weight)
    grad = grad - dot(ordered, cross_high_ref[...], TN) - dot(ordered, cross_low_ref[...], TN)
    for number, (ref, which) in enumerate(((send_ref, 1 - parity), (keep_ref, parity))):
        for i in range(chunks):
            top = number * half + i * share
            for j in range(strips):
                ref[i, j * share : (j + 1) * share, :] = grad[
                    top : top + share, j * lanes : (j + 1) * lanes
                ]
            begin = pl.multiple_of((2 * i + which) * per_owner, per_owner)
            ref[i, body : body + per_owner, :] = grads[pl.ds(begin, per_owner), :]
            ref[i, body + per_owner :, :] = loss


def scale_bits(x):
    top = jnp.max(jnp.abs(x), axis=-2, keepdims=True)
    return jnp.ceil(jnp.log2(jnp.maximum(top, 1e-30)))


def to_code(x):
    return jnp.round(x).astype(jnp.int32).astype(jnp.int16)


def from_code(x):
    return x.astype(jnp.int32).astype(jnp.float32)


def join_kernel(body, per_owner, keep_ref, got_ref, after_ref, out_ref):
    del after_ref
    chunks, _, lanes = keep_ref.shape
    ends = body + 2 * per_owner
    dec = keep_ref[:, :body, :] + got_ref[:, :body, :]
    dec_bits = scale_bits(dec)
    out_ref[:, :body, :] = to_code(dec * (CODE_TOP * jnp.exp2(-dec_bits)))
    rows = slice(body, body + per_owner)
    moved = jnp.concatenate([keep_ref[:, rows, :], got_ref[:, rows, :]], axis=1)
    bits = scale_bits(moved)
    out_ref[:, body:ends, :] = to_code(moved * (CODE_TOP * jnp.exp2(-bits)))
    loss = keep_ref[:, body + per_owner :, :] + got_ref[:, body + per_owner :, :]
    loss = loss[:, :1, :]
    loss_bits = scale_bits(loss)
    loss = loss * (LOSS_TOP * jnp.exp2(-loss_bits))
    high = jnp.round(loss)
    low = (loss - high) * LOSS_TOP
    at = lax.broadcasted_iota(jnp.int32, (chunks, META, lanes), 1)
    meta = jnp.zeros((chunks, META, lanes), jnp.float32)
    for i, value in enumerate((dec_bits, bits, loss_bits, high, low)):
        meta = jnp.where(at == i, value, meta)
    out_ref[:, ends:, :] = to_code(meta)


def place_kernel(parity_ref, request_ref, after_ref, out_ref):
    del after_ref
    peers = request_ref.shape[0]
    rows = request_ref[...][:, 0, :]
    even = jnp.concatenate([rows[d : d + 1, :] for d in range(peers)], axis=1)
    odd = jnp.concatenate([rows[d ^ 1 : (d ^ 1) + 1, :] for d in range(peers)], axis=1)
    wanted = jnp.where(parity_ref[0] == 0, even, odd)
    out_ref[...] = one_hot(lax.broadcasted_iota(jnp.int32, out_ref.shape, 0) == wanted)


def finish_kernel(
    body, per_owner, dec_scale, loss_scale, chosen_ref, got_ref, feat_ref, dec_ref, loss_ref
):
    chunks, _, lanes = got_ref.shape
    share = dec_ref.shape[0]
    ends = body + 2 * per_owner
    meta = from_code(got_ref[:, ends:, :])
    dec = from_code(got_ref[:, :body, :]) * jnp.exp2(meta[:, 0:1, :])
    total = jnp.sum(dec, axis=0) * (dec_scale / CODE_TOP)
    for j in range(body // share):
        dec_ref[:, j * lanes : (j + 1) * lanes] = total[j * share : (j + 1) * share, :]
    loss = (meta[:, 3:4, :] + meta[:, 4:5, :] * (1.0 / LOSS_TOP)) * jnp.exp2(meta[:, 2:3, :])
    loss_ref[...] = jnp.sum(loss, axis=0) * (loss_scale / LOSS_TOP)
    moved = from_code(got_ref[:, body:ends, :]) * (jnp.exp2(meta[:, 1:2, :]) / CODE_TOP)
    high, low = split(moved.reshape(chunks * 2 * per_owner, lanes))
    chosen = chosen_ref[...]
    feat_ref[...] = dot(chosen, high) + dot(chosen, low)


def local(
    features, fetch_ids, tile_lists, depth_order, alpha_codes, list_counts, targets, dec_weight
):
    f32, bf16 = jnp.float32, jnp.bfloat16
    peers = lax.axis_size("wide")
    owned, channels = features.shape
    per_owner = fetch_ids.shape[2]
    rows = peers * per_owner
    tiles, list_len, pixels = alpha_codes.shape
    width = targets.shape[1]
    slots = tiles * list_len
    chunks = peers // 2
    share = channels // peers
    lanes = 128
    body = share * (width // lanes)
    parity = lax.rem(lax.axis_index("wide"), 2)
    shape = jax.ShapeDtypeStruct
    outgoing = pl.pallas_call(
        pick_kernel,
        out_shape=shape((rows, channels), bf16),
        in_specs=[HBM, HBM],
        out_specs=VMEM,
        scratch_shapes=[
            pltpu.VMEM((peers, 1, per_owner), jnp.int32),
            pltpu.VMEM((owned, channels), bf16),
            pltpu.SemaphoreType.DMA((2,)),
        ],
        cost_estimate=pl.CostEstimate(
            flops=20_000_000_000, bytes_accessed=40_000_000, transcendentals=0
        ),
        compiler_params=params(16),
        name="pick",
    )(pin(fetch_ids), pin(features))
    buffer = lax.all_to_all(
        outgoing.reshape(peers, per_owner, channels), "wide", split_axis=0, concat_axis=0, tiled=True
    ).reshape(rows, channels)
    grams = pl.pallas_call(
        gram_kernel,
        out_shape=(
            shape((rows, rows), bf16),
            shape((rows, rows), bf16),
            shape((rows, width), bf16),
            shape((rows, width), bf16),
            shape((rows, channels), f32),
            shape((channels, channels), bf16),
            shape((channels, channels), bf16),
            shape((8, lanes), f32),
        ),
        in_specs=[VMEM] * 5 + [HBM],
        out_specs=(VMEM,) * 8,
        scratch_shapes=[
            pltpu.VMEM((rows, slots), bf16),
            pltpu.VMEM((rows, slots), bf16),
            pltpu.VMEM((rows, slots), bf16),
            pltpu.VMEM((slots, pixels), bf16),
            pltpu.VMEM((slots, width), bf16),
            pltpu.VMEM((slots, width), bf16),
            pltpu.VMEM((tiles * pixels, width), bf16),
            pltpu.VMEM((rows, width), f32),
            pltpu.SemaphoreType.DMA((4,)),
        ],
        cost_estimate=pl.CostEstimate(
            flops=2 * slots * pixels * width + 4 * rows * slots * (width + rows),
            bytes_accessed=targets.size * 2 + alpha_codes.size * 4,
            transcendentals=2 * alpha_codes.size,
        ),
        compiler_params=params(36),
        name="gram",
    )(*map(near, (list_counts, tile_lists, depth_order, dec_weight, alpha_codes)), pin(targets))
    half_shape = shape((chunks, body + per_owner + 8, lanes), f32)
    send, keep = pl.pallas_call(
        gradient_kernel,
        out_shape=(half_shape, half_shape),
        in_specs=[SMEM] + [VMEM] * 10,
        out_specs=(VMEM, VMEM),
        scratch_shapes=[pltpu.VMEM((rows, channels), f32)],
        compiler_params=params(24),
        name="gradient",
    )(parity.reshape(1), buffer, *grams, dec_weight)
    got = lax.ppermute(send, "wide", [(i, i ^ 1) for i in range(peers)])
    chosen = pl.pallas_call(
        place_kernel,
        out_shape=shape((owned, rows), bf16),
        in_specs=[SMEM, VMEM, ANY],
        out_specs=VMEM,
        cost_estimate=pl.CostEstimate(
            flops=owned * rows, bytes_accessed=2 * owned * rows, transcendentals=0
        ),
        compiler_params=params(32),
        name="place",
    )(parity.reshape(1), fetch_ids, send)
    joined = pl.pallas_call(
        functools.partial(join_kernel, body, per_owner),
        out_shape=shape((chunks, body + 2 * per_owner + META, lanes), jnp.int16),
        in_specs=[VMEM, VMEM, ANY],
        out_specs=VMEM,
        compiler_params=params(32),
        name="join",
    )(keep, got, chosen)
    returned = lax.all_to_all(
        joined,
        "wide",
        split_axis=0,
        concat_axis=0,
        axis_index_groups=[[2 * i + c for i in range(chunks)] for c in range(2)],
        tiled=True,
    )
    pixel_total = peers * tiles * pixels
    feat_grad, dec_grad, loss = pl.pallas_call(
        functools.partial(
            finish_kernel,
            body,
            per_owner,
            1.0 / math.sqrt(pixel_total),
            0.5 / (pixel_total * width),
        ),
        out_shape=(
            shape((owned, channels), f32),
            shape((share, width), f32),
            shape((1, lanes), f32),
        ),
        in_specs=[VMEM, VMEM],
        out_specs=(VMEM,) * 3,
        compiler_params=params(32),
        name="finish",
    )(chosen, returned)
    return (feat_grad, dec_grad, loss[0, :1])


def solution(mesh):
    return jax.shard_map(
        local,
        mesh=mesh,
        in_specs=(
            P(("groups", "wide"), None),
            P("groups", "wide", None),
            P(("groups", "wide"), None),
            P(("groups", "wide"), None),
            P(("groups", "wide"), None, None),
            P(("groups", "wide"), None),
            P(("groups", "wide"), None),
            P(),
        ),
        out_specs=(P(("groups", "wide"), None), P(("groups", "wide"), None), P("groups")),
        check_vma=False,
    )
```

```python
import functools
import math

import jax
import jax.numpy as jnp
from jax import lax
from jax.experimental import pallas as pl
from jax.experimental.pallas import tpu as pltpu
from jax.sharding import PartitionSpec as P

ALPHA_TOP = 0.1
NN = (((1,), (0,)), ((), ()))
NT = (((1,), (1,)), ((), ()))
TN = (((0,), (0,)), ((), ()))
VMEM = pl.BlockSpec(memory_space=pltpu.VMEM)
SMEM = pl.BlockSpec(memory_space=pltpu.SMEM)
ANY = pl.BlockSpec(memory_space=pl.ANY)
HBM = pl.BlockSpec(memory_space=pltpu.HBM)
CODE_TOP = 32000.0
LOSS_TOP = 16384.0
META = 16


def dot(a, b, dims=NN):
    return lax.dot_general(a, b, dims, preferred_element_type=jnp.float32)


def split(x):
    high = x.astype(jnp.bfloat16)
    return high, (x - high.astype(jnp.float32)).astype(jnp.bfloat16)


def one_hot(condition):
    return jnp.where(condition, 1.0, 0.0).astype(jnp.bfloat16)


def pin(x):
    return pltpu.with_memory_space_constraint(x, pltpu.HBM)


def near(x):
    return pltpu.with_memory_space_constraint(x, pltpu.VMEM)


def turn(i, chunks):
    return (chunks - 1 - i) ^ 1


def params(mib):
    return pltpu.CompilerParams(vmem_limit_bytes=mib << 20)


def pick_kernel(request_hbm, feature_hbm, out_ref, wanted, held, sems):
    copies = [
        pltpu.make_async_copy(request_hbm, wanted, sems.at[0]),
        pltpu.make_async_copy(feature_hbm, held, sems.at[1]),
    ]
    for copy in copies:
        copy.start()
    peers, _, per_owner = wanted.shape
    owned = held.shape[0]
    lane = lax.broadcasted_iota(jnp.int32, (peers, per_owner, owned), 2)
    copies[0].wait()
    chosen = jnp.where(wanted[...][:, 0, :][:, :, None] == lane, 1.0, 0.0)
    chosen = chosen.reshape(peers * per_owner, owned).astype(jnp.bfloat16)
    copies[1].wait()
    out_ref[...] = dot(chosen, held[...]).astype(jnp.bfloat16)


def gram_kernel(
    count_ref,
    list_ref,
    order_ref,
    weight_ref,
    code_ref,
    target_hbm,
    gram_high_ref,
    gram_low_ref,
    cross_high_ref,
    cross_low_ref,
    back_ref,
    square_high_ref,
    square_low_ref,
    loss_ref,
    hot,
    part_high,
    part_low,
    blends,
    bt_high,
    bt_low,
    target,
    cross,
    sems,
):
    tiles, list_len, pixels = code_ref.shape
    rows = gram_high_ref.shape[0]
    both = 2 * list_len
    pairs = tiles // 2
    part = pairs // 2
    copies = []
    for i, first in enumerate((0, pairs, part, pairs + part)):
        span = pl.ds(first * pixels, part * pixels)
        copies.append(pltpu.make_async_copy(target_hbm.at[span], target.at[span], sems.at[i]))
    for copy in copies:
        copy.start()
    row = lax.broadcasted_iota(jnp.int32, (both, both), 0)
    lane = lax.broadcasted_iota(jnp.int32, (both, both), 1)
    same = (row >= list_len) == (lane >= list_len)
    steps = lane.astype(jnp.float32)
    slot = lax.broadcasted_iota(jnp.int32, (both, 1), 0)
    place = lax.broadcasted_iota(jnp.int32, (rows, both), 0)
    order = jnp.concatenate([order_ref[:pairs, :], order_ref[pairs:, :] + list_len], axis=1)
    listed = jnp.concatenate([list_ref[:pairs, :], list_ref[pairs:, :]], axis=1)
    weight = weight_ref[...]
    high, low = split(dot(weight, weight, NT))
    square_high_ref[...] = high
    square_low_ref[...] = low
    ranks, nearer = [], []
    for i in range(pairs):
        at = row == order[i : i + 1, :]
        rank = jnp.sum(jnp.where(at, steps, 0.0), axis=1, keepdims=True)
        ahead = same & (steps < rank)
        ranks.append(rank)
        nearer.append(dot(one_hot(ahead), one_hot(at), NT).astype(jnp.bfloat16))
    values = []
    for i in range(pairs):
        code = jnp.concatenate([code_ref[i], code_ref[i + pairs]], axis=0)
        alpha = code.astype(jnp.float32) * (ALPHA_TOP / 255.0)
        logs = jnp.concatenate(split(jnp.log(1.0 - alpha)), axis=0)
        transmit = jnp.exp(dot(jnp.concatenate([nearer[i]] * 2, axis=1), logs))
        first = count_ref[:, i : i + 1]
        second = count_ref[:, i + pairs : i + pairs + 1] + list_len
        limit = jnp.where(slot < list_len, first, second)
        live = ranks[i] < limit.astype(jnp.float32)
        blend = jnp.where(live, transmit * alpha, 0.0).astype(jnp.bfloat16)
        blends[i * both : (i + 1) * both, :] = blend
        values.append(blend)
    inner = [split(jnp.where(same, dot(v, v, NT), 0.0)) for v in values]
    for i in range(pairs):
        own = slice(i * both, (i + 1) * both)
        chosen = one_hot(listed[i : i + 1, :] == place)
        hot[:, own] = chosen
        wide = dot(chosen, jnp.concatenate(inner[i], axis=1))
        high, low = split(wide[:, :both] + wide[:, both:])
        part_high[:, own] = high
        part_low[:, own] = low
    chosen = hot[...]
    high, low = split(dot(part_high[...], chosen, NT) + dot(part_low[...], chosen, NT))
    gram_high_ref[...] = high
    gram_low_ref[...] = low
    total = jnp.zeros((8, target.shape[1]), jnp.float32)
    for half in range(2):
        copies[2 * half].wait()
        copies[2 * half + 1].wait()
        for i in range(half * part, (half + 1) * part):
            for side in range(2):
                t = i + side * pairs
                goal = target[t * pixels : (t + 1) * pixels, :]
                begin = i * both + side * list_len
                own = slice(begin, begin + list_len)
                high, low = split(dot(blends[own, :], goal))
                bt_high[own, :] = high
                bt_low[own, :] = low
                wide = goal.astype(jnp.float32)
                total = total + jnp.sum((wide * wide).reshape(pixels // 8, 8, -1), axis=0)
        own = slice(half * part * both, (half + 1) * part * both)
        chosen = hot[:, own]
        more = dot(chosen, bt_high[own, :]) + dot(chosen, bt_low[own, :])
        if half == 0:
            cross[...] = more
    loss_ref[...] = jnp.full(loss_ref.shape, jnp.sum(total), jnp.float32)
    high, low = split(cross[...] + more)
    cross_high_ref[...] = high
    cross_low_ref[...] = low
    back_ref[...] = dot(high, weight, NT) + dot(low, weight, NT)


def gradient_kernel(
    parity_ref,
    buffer_ref,
    gram_high_ref,
    gram_low_ref,
    cross_high_ref,
    cross_low_ref,
    back_ref,
    square_high_ref,
    square_low_ref,
    loss_ref,
    weight_ref,
    send_ref,
    keep_ref,
    grads,
):
    parity = parity_ref[0]
    buffer = buffer_ref[...]
    rows, channels = buffer.shape
    chunks = send_ref.shape[0]
    per_owner = rows // (2 * chunks)
    share = channels // (2 * chunks)
    lanes = 128
    width = weight_ref.shape[1]
    strips = width // lanes
    body = share * strips
    half = channels // 2
    mixed = dot(gram_high_ref[...], buffer) + dot(gram_low_ref[...], buffer)
    high, low = split(mixed)
    square_high = square_high_ref[...]
    back = back_ref[...]
    slope = dot(high, square_high) + dot(low, square_high) + dot(high, square_low_ref[...]) - back
    grads[...] = slope
    loss = loss_ref[...] + jnp.sum(buffer.astype(jnp.float32) * (slope - back))
    source = lax.broadcasted_iota(jnp.int32, (channels, channels), 0)
    goal = lax.broadcasted_iota(jnp.int32, (channels, channels), 1)
    second = goal >= half
    inner = jnp.where(second, goal - half, goal)
    side = jnp.where(second, parity, 1 - parity)
    chunk = inner // share
    wanted = turn(chunk, chunks) * (2 * share) + side * share + (inner - chunk * share)
    ordered = dot(buffer, one_hot(source == wanted)).astype(jnp.bfloat16)
    core_high, core_low = split(dot(ordered, high, TN) + dot(ordered, low, TN))
    weight = weight_ref[...]
    grad = dot(core_high, weight) + dot(core_low, weight)
    grad = grad - dot(ordered, cross_high_ref[...], TN) - dot(ordered, cross_low_ref[...], TN)
    for number, (ref, which) in enumerate(((send_ref, 1 - parity), (keep_ref, parity))):
        for i in range(chunks):
            top = number * half + i * share
            for j in range(strips):
                ref[i, j * share : (j + 1) * share, :] = grad[
                    top : top + share, j * lanes : (j + 1) * lanes
                ]
            begin = pl.multiple_of((2 * turn(i, chunks) + which) * per_owner, per_owner)
            ref[i, body : body + per_owner, :] = grads[pl.ds(begin, per_owner), :]
            ref[i, body + per_owner :, :] = loss


def scale_bits(x):
    top = jnp.max(jnp.abs(x), axis=-2, keepdims=True)
    return jnp.ceil(jnp.log2(jnp.maximum(top, 1e-30)))


def to_code(x):
    return jnp.round(x).astype(jnp.int32).astype(jnp.int16)


def from_code(x):
    return x.astype(jnp.int32).astype(jnp.float32)


def join_kernel(body, per_owner, keep_ref, got_ref, after_ref, out_ref):
    del after_ref
    chunks, _, lanes = keep_ref.shape
    ends = body + 2 * per_owner
    dec = keep_ref[:, :body, :] + got_ref[:, :body, :]
    dec_bits = scale_bits(dec)
    out_ref[:, :body, :] = to_code(dec * (CODE_TOP * jnp.exp2(-dec_bits)))
    rows = slice(body, body + per_owner)
    moved = jnp.concatenate([keep_ref[:, rows, :], got_ref[:, rows, :]], axis=1)
    bits = scale_bits(moved)
    out_ref[:, body:ends, :] = to_code(moved * (CODE_TOP * jnp.exp2(-bits)))
    loss = keep_ref[:, body + per_owner :, :] + got_ref[:, body + per_owner :, :]
    loss = loss[:, :1, :]
    loss_bits = scale_bits(loss)
    loss = loss * (LOSS_TOP * jnp.exp2(-loss_bits))
    high = jnp.round(loss)
    low = (loss - high) * LOSS_TOP
    at = lax.broadcasted_iota(jnp.int32, (chunks, META, lanes), 1)
    meta = jnp.zeros((chunks, META, lanes), jnp.float32)
    for i, value in enumerate((dec_bits, bits, loss_bits, high, low)):
        meta = jnp.where(at == i, value, meta)
    out_ref[:, ends:, :] = to_code(meta)


def place_kernel(parity_ref, request_ref, after_ref, out_ref):
    del after_ref
    peers = request_ref.shape[0]
    rows = request_ref[...][:, 0, :]
    walk = [2 * turn(i, peers // 2) + side for i in range(peers // 2) for side in range(2)]
    even = jnp.concatenate([rows[d : d + 1, :] for d in walk], axis=1)
    odd = jnp.concatenate([rows[d ^ 1 : (d ^ 1) + 1, :] for d in walk], axis=1)
    wanted = jnp.where(parity_ref[0] == 0, even, odd)
    out_ref[...] = one_hot(lax.broadcasted_iota(jnp.int32, out_ref.shape, 0) == wanted)


def finish_kernel(
    body, per_owner, dec_scale, loss_scale, chosen_ref, got_ref, feat_ref, dec_ref, loss_ref
):
    chunks, _, lanes = got_ref.shape
    share = dec_ref.shape[0]
    ends = body + 2 * per_owner
    meta = from_code(got_ref[:, ends:, :])
    dec = from_code(got_ref[:, :body, :]) * jnp.exp2(meta[:, 0:1, :])
    total = jnp.sum(dec, axis=0) * (dec_scale / CODE_TOP)
    for j in range(body // share):
        dec_ref[:, j * lanes : (j + 1) * lanes] = total[j * share : (j + 1) * share, :]
    loss = (meta[:, 3:4, :] + meta[:, 4:5, :] * (1.0 / LOSS_TOP)) * jnp.exp2(meta[:, 2:3, :])
    loss_ref[...] = jnp.sum(loss, axis=0) * (loss_scale / LOSS_TOP)
    moved = from_code(got_ref[:, body:ends, :]) * (jnp.exp2(meta[:, 1:2, :]) / CODE_TOP)
    high, low = split(moved.reshape(chunks * 2 * per_owner, lanes))
    chosen = chosen_ref[...]
    feat_ref[...] = dot(chosen, high) + dot(chosen, low)


def local(
    features, fetch_ids, tile_lists, depth_order, alpha_codes, list_counts, targets, dec_weight
):
    f32, bf16 = jnp.float32, jnp.bfloat16
    peers = lax.axis_size("wide")
    owned, channels = features.shape
    per_owner = fetch_ids.shape[2]
    rows = peers * per_owner
    tiles, list_len, pixels = alpha_codes.shape
    width = targets.shape[1]
    slots = tiles * list_len
    chunks = peers // 2
    share = channels // peers
    lanes = 128
    body = share * (width // lanes)
    parity = lax.rem(lax.axis_index("wide"), 2)
    shape = jax.ShapeDtypeStruct
    outgoing = pl.pallas_call(
        pick_kernel,
        out_shape=shape((rows, channels), bf16),
        in_specs=[HBM, HBM],
        out_specs=VMEM,
        scratch_shapes=[
            pltpu.VMEM((peers, 1, per_owner), jnp.int32),
            pltpu.VMEM((owned, channels), bf16),
            pltpu.SemaphoreType.DMA((2,)),
        ],
        cost_estimate=pl.CostEstimate(
            flops=20_000_000_000, bytes_accessed=40_000_000, transcendentals=0
        ),
        compiler_params=params(16),
        name="pick",
    )(pin(fetch_ids), pin(features))
    buffer = lax.all_to_all(
        outgoing.reshape(peers, per_owner, channels), "wide", split_axis=0, concat_axis=0, tiled=True
    ).reshape(rows, channels)
    grams = pl.pallas_call(
        gram_kernel,
        out_shape=(
            shape((rows, rows), bf16),
            shape((rows, rows), bf16),
            shape((rows, width), bf16),
            shape((rows, width), bf16),
            shape((rows, channels), f32),
            shape((channels, channels), bf16),
            shape((channels, channels), bf16),
            shape((8, lanes), f32),
        ),
        in_specs=[VMEM] * 5 + [HBM],
        out_specs=(VMEM,) * 8,
        scratch_shapes=[
            pltpu.VMEM((rows, slots), bf16),
            pltpu.VMEM((rows, slots), bf16),
            pltpu.VMEM((rows, slots), bf16),
            pltpu.VMEM((slots, pixels), bf16),
            pltpu.VMEM((slots, width), bf16),
            pltpu.VMEM((slots, width), bf16),
            pltpu.VMEM((tiles * pixels, width), bf16),
            pltpu.VMEM((rows, width), f32),
            pltpu.SemaphoreType.DMA((4,)),
        ],
        cost_estimate=pl.CostEstimate(
            flops=2 * slots * pixels * width + 4 * rows * slots * (width + rows),
            bytes_accessed=targets.size * 2 + alpha_codes.size * 4,
            transcendentals=2 * alpha_codes.size,
        ),
        compiler_params=params(36),
        name="gram",
    )(*map(near, (list_counts, tile_lists, depth_order, dec_weight, alpha_codes)), pin(targets))
    half_shape = shape((chunks, body + per_owner + 8, lanes), f32)
    send, keep = pl.pallas_call(
        gradient_kernel,
        out_shape=(half_shape, half_shape),
        in_specs=[SMEM] + [VMEM] * 10,
        out_specs=(VMEM, VMEM),
        scratch_shapes=[pltpu.VMEM((rows, channels), f32)],
        compiler_params=params(24),
        name="gradient",
    )(parity.reshape(1), buffer, *grams, dec_weight)
    got = lax.ppermute(send, "wide", [(i, i ^ 1) for i in range(peers)])
    chosen = pl.pallas_call(
        place_kernel,
        out_shape=shape((owned, rows), bf16),
        in_specs=[SMEM, VMEM, ANY],
        out_specs=VMEM,
        cost_estimate=pl.CostEstimate(
            flops=owned * rows, bytes_accessed=2 * owned * rows, transcendentals=0
        ),
        compiler_params=params(32),
        name="place",
    )(parity.reshape(1), fetch_ids, send)
    joined = pl.pallas_call(
        functools.partial(join_kernel, body, per_owner),
        out_shape=shape((chunks, body + 2 * per_owner + META, lanes), jnp.int16),
        in_specs=[VMEM, VMEM, ANY],
        out_specs=VMEM,
        compiler_params=params(32),
        name="join",
    )(keep, got, chosen)
    returned = lax.all_to_all(
        joined,
        "wide",
        split_axis=0,
        concat_axis=0,
        axis_index_groups=[[2 * turn(i, chunks) + c for i in range(chunks)] for c in range(2)],
        tiled=True,
    )
    pixel_total = peers * tiles * pixels
    feat_grad, dec_grad, loss = pl.pallas_call(
        functools.partial(
            finish_kernel,
            body,
            per_owner,
            1.0 / math.sqrt(pixel_total),
            0.5 / (pixel_total * width),
        ),
        out_shape=(
            shape((owned, channels), f32),
            shape((share, width), f32),
            shape((1, lanes), f32),
        ),
        in_specs=[VMEM, VMEM],
        out_specs=(VMEM,) * 3,
        compiler_params=params(32),
        name="finish",
    )(chosen, returned)
    return (feat_grad, dec_grad, loss[0, :1])


def solution(mesh):
    return jax.shard_map(
        local,
        mesh=mesh,
        in_specs=(
            P(("groups", "wide"), None),
            P("groups", "wide", None),
            P(("groups", "wide"), None),
            P(("groups", "wide"), None),
            P(("groups", "wide"), None, None),
            P(("groups", "wide"), None),
            P(("groups", "wide"), None),
            P(),
        ),
        out_specs=(P(("groups", "wide"), None), P(("groups", "wide"), None), P("groups")),
        check_vma=False,
    )
```

```python
import functools
import math

import jax
import jax.numpy as jnp
from jax import lax
from jax.experimental import pallas as pl
from jax.experimental.pallas import tpu as pltpu
from jax.sharding import PartitionSpec as P

ALPHA_TOP = 0.1
NN = (((1,), (0,)), ((), ()))
NT = (((1,), (1,)), ((), ()))
TN = (((0,), (0,)), ((), ()))
VMEM = pl.BlockSpec(memory_space=pltpu.VMEM)
SMEM = pl.BlockSpec(memory_space=pltpu.SMEM)
ANY = pl.BlockSpec(memory_space=pl.ANY)
HBM = pl.BlockSpec(memory_space=pltpu.HBM)
CODE_TOP = 32000.0
LOSS_TOP = 16384.0
META = 16


def dot(a, b, dims=NN):
    return lax.dot_general(a, b, dims, preferred_element_type=jnp.float32)


def split(x):
    high = x.astype(jnp.bfloat16)
    return high, (x - high.astype(jnp.float32)).astype(jnp.bfloat16)


def one_hot(condition):
    return jnp.where(condition, 1.0, 0.0).astype(jnp.bfloat16)


def pin(x):
    return pltpu.with_memory_space_constraint(x, pltpu.HBM)


def near(x):
    return pltpu.with_memory_space_constraint(x, pltpu.VMEM)


def turn(i, chunks):
    return (chunks - 1 - i) ^ 1


def params(mib):
    return pltpu.CompilerParams(vmem_limit_bytes=mib << 20)


def pick_kernel(request_hbm, feature_hbm, out_ref, wanted, held, sems):
    copies = [
        pltpu.make_async_copy(request_hbm, wanted, sems.at[0]),
        pltpu.make_async_copy(feature_hbm, held, sems.at[1]),
    ]
    for copy in copies:
        copy.start()
    peers, _, per_owner = wanted.shape
    owned = held.shape[0]
    lane = lax.broadcasted_iota(jnp.int32, (peers, per_owner, owned), 2)
    copies[0].wait()
    chosen = jnp.where(wanted[...][:, 0, :][:, :, None] == lane, 1.0, 0.0)
    chosen = chosen.reshape(peers * per_owner, owned).astype(jnp.bfloat16)
    copies[1].wait()
    out_ref[...] = dot(chosen, held[...]).astype(jnp.bfloat16)


def gram_kernel(
    count_ref,
    list_ref,
    order_ref,
    weight_ref,
    code_ref,
    target_hbm,
    gram_high_ref,
    gram_low_ref,
    cross_high_ref,
    cross_low_ref,
    back_ref,
    square_high_ref,
    square_low_ref,
    loss_ref,
    hot,
    part_high,
    part_low,
    blends,
    bt_high,
    bt_low,
    target,
    cross,
    sems,
):
    tiles, list_len, pixels = code_ref.shape
    rows = gram_high_ref.shape[0]
    both = 2 * list_len
    pairs = tiles // 2
    part = pairs // 2
    copies = []
    for i, first in enumerate((0, pairs, part, pairs + part)):
        span = pl.ds(first * pixels, part * pixels)
        copies.append(pltpu.make_async_copy(target_hbm.at[span], target.at[span], sems.at[i]))
    for copy in copies:
        copy.start()
    row = lax.broadcasted_iota(jnp.int32, (both, both), 0)
    lane = lax.broadcasted_iota(jnp.int32, (both, both), 1)
    same = (row >= list_len) == (lane >= list_len)
    steps = lane.astype(jnp.float32)
    slot = lax.broadcasted_iota(jnp.int32, (both, 1), 0)
    place = lax.broadcasted_iota(jnp.int32, (rows, both), 0)
    order = jnp.concatenate([order_ref[:pairs, :], order_ref[pairs:, :] + list_len], axis=1)
    listed = jnp.concatenate([list_ref[:pairs, :], list_ref[pairs:, :]], axis=1)
    weight = weight_ref[...]
    high, low = split(dot(weight, weight, NT))
    square_high_ref[...] = high
    square_low_ref[...] = low
    ranks, nearer = [], []
    for i in range(pairs):
        at = row == order[i : i + 1, :]
        rank = jnp.sum(jnp.where(at, steps, 0.0), axis=1, keepdims=True)
        ahead = same & (steps < rank)
        ranks.append(rank)
        nearer.append(dot(one_hot(ahead), one_hot(at), NT).astype(jnp.bfloat16))
    values = []
    for i in range(pairs):
        code = jnp.concatenate([code_ref[i], code_ref[i + pairs]], axis=0)
        alpha = code.astype(jnp.float32) * (ALPHA_TOP / 255.0)
        logs = jnp.concatenate(split(jnp.log(1.0 - alpha)), axis=0)
        transmit = jnp.exp(dot(jnp.concatenate([nearer[i]] * 2, axis=1), logs))
        first = count_ref[:, i : i + 1]
        second = count_ref[:, i + pairs : i + pairs + 1] + list_len
        limit = jnp.where(slot < list_len, first, second)
        live = ranks[i] < limit.astype(jnp.float32)
        blend = jnp.where(live, transmit * alpha, 0.0).astype(jnp.bfloat16)
        blends[i * both : (i + 1) * both, :] = blend
        values.append(blend)
    inner = [split(jnp.where(same, dot(v, v, NT), 0.0)) for v in values]
    for i in range(pairs):
        own = slice(i * both, (i + 1) * both)
        chosen = one_hot(listed[i : i + 1, :] == place)
        hot[:, own] = chosen
        wide = dot(chosen, jnp.concatenate(inner[i], axis=1))
        high, low = split(wide[:, :both] + wide[:, both:])
        part_high[:, own] = high
        part_low[:, own] = low
    chosen = hot[...]
    high, low = split(dot(part_high[...], chosen, NT) + dot(part_low[...], chosen, NT))
    gram_high_ref[...] = high
    gram_low_ref[...] = low
    total = jnp.zeros((8, target.shape[1]), jnp.float32)
    for half in range(2):
        copies[2 * half].wait()
        copies[2 * half + 1].wait()
        for i in range(half * part, (half + 1) * part):
            for side in range(2):
                t = i + side * pairs
                goal = target[t * pixels : (t + 1) * pixels, :]
                begin = i * both + side * list_len
                own = slice(begin, begin + list_len)
                high, low = split(dot(blends[own, :], goal))
                bt_high[own, :] = high
                bt_low[own, :] = low
                wide = goal.astype(jnp.float32)
                total = total + jnp.sum((wide * wide).reshape(pixels // 8, 8, -1), axis=0)
        own = slice(half * part * both, (half + 1) * part * both)
        chosen = hot[:, own]
        more = dot(chosen, bt_high[own, :]) + dot(chosen, bt_low[own, :])
        if half == 0:
            cross[...] = more
    loss_ref[...] = jnp.full(loss_ref.shape, jnp.sum(total), jnp.float32)
    high, low = split(cross[...] + more)
    cross_high_ref[...] = high
    cross_low_ref[...] = low
    back_ref[...] = dot(high, weight, NT) + dot(low, weight, NT)


def gradient_kernel(
    parity_ref,
    buffer_ref,
    gram_high_ref,
    gram_low_ref,
    cross_high_ref,
    cross_low_ref,
    back_ref,
    square_high_ref,
    square_low_ref,
    loss_ref,
    weight_ref,
    send_ref,
    keep_ref,
    grads,
):
    parity = parity_ref[0]
    buffer = buffer_ref[...]
    rows, channels = buffer.shape
    chunks = send_ref.shape[0]
    per_owner = rows // (2 * chunks)
    share = channels // (2 * chunks)
    lanes = 128
    width = weight_ref.shape[1]
    strips = width // lanes
    body = share * strips
    half = channels // 2
    mixed = dot(gram_high_ref[...], buffer) + dot(gram_low_ref[...], buffer)
    high, low = split(mixed)
    square_high = square_high_ref[...]
    back = back_ref[...]
    slope = dot(high, square_high) + dot(low, square_high) + dot(high, square_low_ref[...]) - back
    grads[...] = slope
    loss = loss_ref[...] + jnp.sum(buffer.astype(jnp.float32) * (slope - back))
    source = lax.broadcasted_iota(jnp.int32, (channels, channels), 0)
    goal = lax.broadcasted_iota(jnp.int32, (channels, channels), 1)
    second = goal >= half
    inner = jnp.where(second, goal - half, goal)
    side = jnp.where(second, parity, 1 - parity)
    chunk = inner // share
    wanted = turn(chunk, chunks) * (2 * share) + side * share + (inner - chunk * share)
    ordered = dot(buffer, one_hot(source == wanted)).astype(jnp.bfloat16)
    core_high, core_low = split(dot(ordered, high, TN) + dot(ordered, low, TN))
    weight = weight_ref[...]
    grad = dot(core_high, weight) + dot(core_low, weight)
    grad = grad - dot(ordered, cross_high_ref[...], TN) - dot(ordered, cross_low_ref[...], TN)
    for number, (ref, which) in enumerate(((send_ref, 1 - parity), (keep_ref, parity))):
        for i in range(chunks):
            top = number * half + i * share
            for j in range(strips):
                ref[i, j * share : (j + 1) * share, :] = grad[
                    top : top + share, j * lanes : (j + 1) * lanes
                ]
            begin = pl.multiple_of((2 * turn(i, chunks) + which) * per_owner, per_owner)
            ref[i, body : body + per_owner, :] = grads[pl.ds(begin, per_owner), :]
            ref[i, body + per_owner :, :] = loss


def scale_bits(x):
    top = jnp.max(jnp.abs(x), axis=-2, keepdims=True)
    return jnp.ceil(jnp.log2(jnp.maximum(top, 1e-30)))


def to_code(x):
    return jnp.round(x).astype(jnp.int32).astype(jnp.int16)


def from_code(x):
    return x.astype(jnp.int32).astype(jnp.float32)


def join_kernel(body, per_owner, keep_ref, got_ref, after_ref, out_ref):
    del after_ref
    chunks, _, lanes = keep_ref.shape
    ends = body + 2 * per_owner
    dec = keep_ref[:, :body, :] + got_ref[:, :body, :]
    dec_bits = scale_bits(dec)
    out_ref[:, :body, :] = to_code(dec * (CODE_TOP * jnp.exp2(-dec_bits)))
    rows = slice(body, body + per_owner)
    moved = jnp.concatenate([keep_ref[:, rows, :], got_ref[:, rows, :]], axis=1)
    bits = scale_bits(moved)
    out_ref[:, body:ends, :] = to_code(moved * (CODE_TOP * jnp.exp2(-bits)))
    loss = keep_ref[:, body + per_owner :, :] + got_ref[:, body + per_owner :, :]
    loss = loss[:, :1, :]
    loss_bits = scale_bits(loss)
    loss = loss * (LOSS_TOP * jnp.exp2(-loss_bits))
    high = jnp.round(loss)
    low = (loss - high) * LOSS_TOP
    at = lax.broadcasted_iota(jnp.int32, (chunks, META, lanes), 1)
    meta = jnp.zeros((chunks, META, lanes), jnp.float32)
    for i, value in enumerate((dec_bits, bits, loss_bits, high, low)):
        meta = jnp.where(at == i, value, meta)
    out_ref[:, ends:, :] = to_code(meta)


def place_kernel(parity_ref, request_ref, after_ref, out_ref):
    del after_ref
    peers = request_ref.shape[0]
    rows = request_ref[...][:, 0, :]
    walk = [2 * turn(i, peers // 2) + side for i in range(peers // 2) for side in range(2)]
    even = jnp.concatenate([rows[d : d + 1, :] for d in walk], axis=1)
    odd = jnp.concatenate([rows[d ^ 1 : (d ^ 1) + 1, :] for d in walk], axis=1)
    wanted = jnp.where(parity_ref[0] == 0, even, odd)
    out_ref[...] = one_hot(lax.broadcasted_iota(jnp.int32, out_ref.shape, 0) == wanted)


def finish_kernel(
    body,
    per_owner,
    dec_scale,
    loss_scale,
    chosen_ref,
    got_ref,
    feat_hbm,
    dec_hbm,
    loss_hbm,
    feat,
    dec,
    loss,
    sems,
):
    chunks, _, lanes = got_ref.shape
    share = dec.shape[0]
    ends = body + 2 * per_owner
    meta = from_code(got_ref[:, ends:, :])
    moved = from_code(got_ref[:, body:ends, :]) * (jnp.exp2(meta[:, 1:2, :]) / CODE_TOP)
    high, low = split(moved.reshape(chunks * 2 * per_owner, lanes))
    blocks = sems.shape[0] - 2
    step = feat.shape[0] // blocks
    copies = []
    for i in range(blocks):
        own = slice(i * step, (i + 1) * step)
        chosen = chosen_ref[own, :]
        feat[own, :] = dot(chosen, high) + dot(chosen, low)
        span = pl.ds(i * step, step)
        copies.append(pltpu.make_async_copy(feat.at[span], feat_hbm.at[span], sems.at[i]))
        copies[-1].start()
    parts = from_code(got_ref[:, :body, :]) * jnp.exp2(meta[:, 0:1, :])
    total = jnp.sum(parts, axis=0) * (dec_scale / CODE_TOP)
    for j in range(body // share):
        dec[:, j * lanes : (j + 1) * lanes] = total[j * share : (j + 1) * share, :]
    copies.append(pltpu.make_async_copy(dec, dec_hbm, sems.at[blocks]))
    copies[-1].start()
    sums = (meta[:, 3:4, :] + meta[:, 4:5, :] * (1.0 / LOSS_TOP)) * jnp.exp2(meta[:, 2:3, :])
    loss[...] = jnp.sum(sums, axis=0) * (loss_scale / LOSS_TOP)
    copies.append(pltpu.make_async_copy(loss, loss_hbm, sems.at[blocks + 1]))
    copies[-1].start()
    for copy in copies:
        copy.wait()


def local(
    features, fetch_ids, tile_lists, depth_order, alpha_codes, list_counts, targets, dec_weight
):
    f32, bf16 = jnp.float32, jnp.bfloat16
    peers = lax.axis_size("wide")
    owned, channels = features.shape
    per_owner = fetch_ids.shape[2]
    rows = peers * per_owner
    tiles, list_len, pixels = alpha_codes.shape
    width = targets.shape[1]
    slots = tiles * list_len
    chunks = peers // 2
    share = channels // peers
    lanes = 128
    body = share * (width // lanes)
    parity = lax.rem(lax.axis_index("wide"), 2)
    shape = jax.ShapeDtypeStruct
    outgoing = pl.pallas_call(
        pick_kernel,
        out_shape=shape((rows, channels), bf16),
        in_specs=[HBM, HBM],
        out_specs=VMEM,
        scratch_shapes=[
            pltpu.VMEM((peers, 1, per_owner), jnp.int32),
            pltpu.VMEM((owned, channels), bf16),
            pltpu.SemaphoreType.DMA((2,)),
        ],
        cost_estimate=pl.CostEstimate(
            flops=20_000_000_000, bytes_accessed=40_000_000, transcendentals=0
        ),
        compiler_params=params(16),
        name="pick",
    )(pin(fetch_ids), pin(features))
    buffer = lax.all_to_all(
        outgoing.reshape(peers, per_owner, channels), "wide", split_axis=0, concat_axis=0, tiled=True
    ).reshape(rows, channels)
    grams = pl.pallas_call(
        gram_kernel,
        out_shape=(
            shape((rows, rows), bf16),
            shape((rows, rows), bf16),
            shape((rows, width), bf16),
            shape((rows, width), bf16),
            shape((rows, channels), f32),
            shape((channels, channels), bf16),
            shape((channels, channels), bf16),
            shape((8, lanes), f32),
        ),
        in_specs=[VMEM] * 5 + [HBM],
        out_specs=(VMEM,) * 8,
        scratch_shapes=[
            pltpu.VMEM((rows, slots), bf16),
            pltpu.VMEM((rows, slots), bf16),
            pltpu.VMEM((rows, slots), bf16),
            pltpu.VMEM((slots, pixels), bf16),
            pltpu.VMEM((slots, width), bf16),
            pltpu.VMEM((slots, width), bf16),
            pltpu.VMEM((tiles * pixels, width), bf16),
            pltpu.VMEM((rows, width), f32),
            pltpu.SemaphoreType.DMA((4,)),
        ],
        cost_estimate=pl.CostEstimate(
            flops=2 * slots * pixels * width + 4 * rows * slots * (width + rows),
            bytes_accessed=targets.size * 2 + alpha_codes.size * 4,
            transcendentals=2 * alpha_codes.size,
        ),
        compiler_params=params(36),
        name="gram",
    )(*map(near, (list_counts, tile_lists, depth_order, dec_weight, alpha_codes)), pin(targets))
    half_shape = shape((chunks, body + per_owner + 8, lanes), f32)
    send, keep = pl.pallas_call(
        gradient_kernel,
        out_shape=(half_shape, half_shape),
        in_specs=[SMEM] + [VMEM] * 10,
        out_specs=(VMEM, VMEM),
        scratch_shapes=[pltpu.VMEM((rows, channels), f32)],
        compiler_params=params(24),
        name="gradient",
    )(parity.reshape(1), buffer, *grams, dec_weight)
    got = lax.ppermute(send, "wide", [(i, i ^ 1) for i in range(peers)])
    chosen = pl.pallas_call(
        place_kernel,
        out_shape=shape((owned, rows), bf16),
        in_specs=[SMEM, VMEM, ANY],
        out_specs=VMEM,
        cost_estimate=pl.CostEstimate(
            flops=owned * rows, bytes_accessed=2 * owned * rows, transcendentals=0
        ),
        compiler_params=params(32),
        name="place",
    )(parity.reshape(1), fetch_ids, send)
    joined = pl.pallas_call(
        functools.partial(join_kernel, body, per_owner),
        out_shape=shape((chunks, body + 2 * per_owner + META, lanes), jnp.int16),
        in_specs=[VMEM, VMEM, ANY],
        out_specs=VMEM,
        compiler_params=params(32),
        name="join",
    )(keep, got, chosen)
    returned = lax.all_to_all(
        joined,
        "wide",
        split_axis=0,
        concat_axis=0,
        axis_index_groups=[[2 * turn(i, chunks) + c for i in range(chunks)] for c in range(2)],
        tiled=True,
    )
    pixel_total = peers * tiles * pixels
    feat_grad, dec_grad, loss = pl.pallas_call(
        functools.partial(
            finish_kernel,
            body,
            per_owner,
            1.0 / math.sqrt(pixel_total),
            0.5 / (pixel_total * width),
        ),
        out_shape=(
            shape((owned, channels), f32),
            shape((share, width), f32),
            shape((1, lanes), f32),
        ),
        in_specs=[VMEM, VMEM],
        out_specs=(HBM,) * 3,
        scratch_shapes=[
            pltpu.VMEM((owned, channels), f32),
            pltpu.VMEM((share, width), f32),
            pltpu.VMEM((1, lanes), f32),
            pltpu.SemaphoreType.DMA((6,)),
        ],
        compiler_params=params(32),
        name="finish",
    )(chosen, returned)
    return (feat_grad, dec_grad, loss[0, :1])


def solution(mesh):
    return jax.shard_map(
        local,
        mesh=mesh,
        in_specs=(
            P(("groups", "wide"), None),
            P("groups", "wide", None),
            P(("groups", "wide"), None),
            P(("groups", "wide"), None),
            P(("groups", "wide"), None, None),
            P(("groups", "wide"), None),
            P(("groups", "wide"), None),
            P(),
        ),
        out_specs=(P(("groups", "wide"), None), P(("groups", "wide"), None), P("groups")),
        check_vma=False,
    )
```

```python
import functools
import math

import jax
import jax.numpy as jnp
from jax import lax
from jax.experimental import pallas as pl
from jax.experimental.pallas import tpu as pltpu
from jax.sharding import PartitionSpec as P

ALPHA_TOP = 0.1
NN = (((1,), (0,)), ((), ()))
NT = (((1,), (1,)), ((), ()))
TN = (((0,), (0,)), ((), ()))
VMEM = pl.BlockSpec(memory_space=pltpu.VMEM)
SMEM = pl.BlockSpec(memory_space=pltpu.SMEM)
ANY = pl.BlockSpec(memory_space=pl.ANY)
HBM = pl.BlockSpec(memory_space=pltpu.HBM)
CODE_TOP = 32000.0
LOSS_TOP = 16384.0
META = 16


def dot(a, b, dims=NN):
    return lax.dot_general(a, b, dims, preferred_element_type=jnp.float32)


def split(x):
    high = x.astype(jnp.bfloat16)
    return high, (x - high.astype(jnp.float32)).astype(jnp.bfloat16)


def one_hot(condition):
    return jnp.where(condition, 1.0, 0.0).astype(jnp.bfloat16)


def pin(x):
    return pltpu.with_memory_space_constraint(x, pltpu.HBM)


def near(x):
    return pltpu.with_memory_space_constraint(x, pltpu.VMEM)


def turn(i, chunks):
    return (chunks - 1 - i) ^ 1


def params(mib):
    return pltpu.CompilerParams(vmem_limit_bytes=mib << 20)


def pick_kernel(request_hbm, feature_hbm, out_hbm, wanted, held, picked, sems):
    copies = [
        pltpu.make_async_copy(request_hbm, wanted, sems.at[0]),
        pltpu.make_async_copy(feature_hbm, held, sems.at[1]),
    ]
    for copy in copies:
        copy.start()
    peers, _, per_owner = wanted.shape
    owned = held.shape[0]
    lane = lax.broadcasted_iota(jnp.int32, (peers, per_owner, owned), 2)
    copies[0].wait()
    chosen = jnp.where(wanted[...][:, 0, :][:, :, None] == lane, 1.0, 0.0)
    chosen = chosen.reshape(peers * per_owner, owned).astype(jnp.bfloat16)
    copies[1].wait()
    half = picked.shape[0] // 2
    for i in range(2):
        own = slice(i * half, (i + 1) * half)
        picked[own, :] = dot(chosen[own], held[...]).astype(jnp.bfloat16)
        span = pl.ds(i * half, half)
        copies.append(
            pltpu.make_async_copy(picked.at[span], out_hbm.at[span], sems.at[2 + i])
        )
        copies[-1].start()
    for copy in copies[2:]:
        copy.wait()


def gram_kernel(
    count_ref,
    list_ref,
    order_ref,
    weight_ref,
    code_ref,
    target_hbm,
    gram_high_ref,
    gram_low_ref,
    cross_high_ref,
    cross_low_ref,
    back_ref,
    square_high_ref,
    square_low_ref,
    loss_ref,
    hot,
    part_high,
    part_low,
    blends,
    bt_high,
    bt_low,
    target,
    cross,
    sems,
):
    tiles, list_len, pixels = code_ref.shape
    rows = gram_high_ref.shape[0]
    both = 2 * list_len
    pairs = tiles // 2
    part = pairs // 2
    copies = []
    for i, first in enumerate((0, pairs, part, pairs + part)):
        span = pl.ds(first * pixels, part * pixels)
        copies.append(pltpu.make_async_copy(target_hbm.at[span], target.at[span], sems.at[i]))
    for copy in copies:
        copy.start()
    row = lax.broadcasted_iota(jnp.int32, (both, both), 0)
    lane = lax.broadcasted_iota(jnp.int32, (both, both), 1)
    same = (row >= list_len) == (lane >= list_len)
    steps = lane.astype(jnp.float32)
    slot = lax.broadcasted_iota(jnp.int32, (both, 1), 0)
    place = lax.broadcasted_iota(jnp.int32, (rows, both), 0)
    order = jnp.concatenate([order_ref[:pairs, :], order_ref[pairs:, :] + list_len], axis=1)
    listed = jnp.concatenate([list_ref[:pairs, :], list_ref[pairs:, :]], axis=1)
    weight = weight_ref[...]
    high, low = split(dot(weight, weight, NT))
    square_high_ref[...] = high
    square_low_ref[...] = low
    ranks, nearer = [], []
    for i in range(pairs):
        at = row == order[i : i + 1, :]
        rank = jnp.sum(jnp.where(at, steps, 0.0), axis=1, keepdims=True)
        ahead = same & (steps < rank)
        ranks.append(rank)
        nearer.append(dot(one_hot(ahead), one_hot(at), NT).astype(jnp.bfloat16))
    values = []
    for i in range(pairs):
        code = jnp.concatenate([code_ref[i], code_ref[i + pairs]], axis=0)
        alpha = code.astype(jnp.float32) * (ALPHA_TOP / 255.0)
        logs = jnp.concatenate(split(jnp.log(1.0 - alpha)), axis=0)
        transmit = jnp.exp(dot(jnp.concatenate([nearer[i]] * 2, axis=1), logs))
        first = count_ref[:, i : i + 1]
        second = count_ref[:, i + pairs : i + pairs + 1] + list_len
        limit = jnp.where(slot < list_len, first, second)
        live = ranks[i] < limit.astype(jnp.float32)
        blend = jnp.where(live, transmit * alpha, 0.0).astype(jnp.bfloat16)
        blends[i * both : (i + 1) * both, :] = blend
        values.append(blend)
    inner = [split(jnp.where(same, dot(v, v, NT), 0.0)) for v in values]
    for i in range(pairs):
        own = slice(i * both, (i + 1) * both)
        chosen = one_hot(listed[i : i + 1, :] == place)
        hot[:, own] = chosen
        wide = dot(chosen, jnp.concatenate(inner[i], axis=1))
        high, low = split(wide[:, :both] + wide[:, both:])
        part_high[:, own] = high
        part_low[:, own] = low
    chosen = hot[...]
    high, low = split(dot(part_high[...], chosen, NT) + dot(part_low[...], chosen, NT))
    gram_high_ref[...] = high
    gram_low_ref[...] = low
    total = jnp.zeros((8, target.shape[1]), jnp.float32)
    for half in range(2):
        copies[2 * half].wait()
        copies[2 * half + 1].wait()
        for i in range(half * part, (half + 1) * part):
            for side in range(2):
                t = i + side * pairs
                goal = target[t * pixels : (t + 1) * pixels, :]
                begin = i * both + side * list_len
                own = slice(begin, begin + list_len)
                high, low = split(dot(blends[own, :], goal))
                bt_high[own, :] = high
                bt_low[own, :] = low
                wide = goal.astype(jnp.float32)
                total = total + jnp.sum((wide * wide).reshape(pixels // 8, 8, -1), axis=0)
        own = slice(half * part * both, (half + 1) * part * both)
        chosen = hot[:, own]
        more = dot(chosen, bt_high[own, :]) + dot(chosen, bt_low[own, :])
        if half == 0:
            cross[...] = more
    loss_ref[...] = jnp.full(loss_ref.shape, jnp.sum(total), jnp.float32)
    high, low = split(cross[...] + more)
    cross_high_ref[...] = high
    cross_low_ref[...] = low
    back_ref[...] = dot(high, weight, NT) + dot(low, weight, NT)


def gradient_kernel(
    parity_ref,
    buffer_ref,
    gram_high_ref,
    gram_low_ref,
    cross_high_ref,
    cross_low_ref,
    back_ref,
    square_high_ref,
    square_low_ref,
    loss_ref,
    weight_ref,
    send_ref,
    keep_ref,
    grads,
):
    parity = parity_ref[0]
    buffer = buffer_ref[...]
    rows, channels = buffer.shape
    chunks = send_ref.shape[0]
    per_owner = rows // (2 * chunks)
    share = channels // (2 * chunks)
    lanes = 128
    width = weight_ref.shape[1]
    strips = width // lanes
    body = share * strips
    half = channels // 2
    mixed = dot(gram_high_ref[...], buffer) + dot(gram_low_ref[...], buffer)
    high, low = split(mixed)
    square_high = square_high_ref[...]
    back = back_ref[...]
    slope = dot(high, square_high) + dot(low, square_high) + dot(high, square_low_ref[...]) - back
    grads[...] = slope
    loss = loss_ref[...] + jnp.sum(buffer.astype(jnp.float32) * (slope - back))
    source = lax.broadcasted_iota(jnp.int32, (channels, channels), 0)
    goal = lax.broadcasted_iota(jnp.int32, (channels, channels), 1)
    second = goal >= half
    inner = jnp.where(second, goal - half, goal)
    side = jnp.where(second, parity, 1 - parity)
    chunk = inner // share
    wanted = turn(chunk, chunks) * (2 * share) + side * share + (inner - chunk * share)
    ordered = dot(buffer, one_hot(source == wanted)).astype(jnp.bfloat16)
    core_high, core_low = split(dot(ordered, high, TN) + dot(ordered, low, TN))
    weight = weight_ref[...]
    grad = dot(core_high, weight) + dot(core_low, weight)
    grad = grad - dot(ordered, cross_high_ref[...], TN) - dot(ordered, cross_low_ref[...], TN)
    for number, (ref, which) in enumerate(((send_ref, 1 - parity), (keep_ref, parity))):
        for i in range(chunks):
            top = number * half + i * share
            for j in range(strips):
                ref[i, j * share : (j + 1) * share, :] = grad[
                    top : top + share, j * lanes : (j + 1) * lanes
                ]
            begin = pl.multiple_of((2 * turn(i, chunks) + which) * per_owner, per_owner)
            ref[i, body : body + per_owner, :] = grads[pl.ds(begin, per_owner), :]
            ref[i, body + per_owner :, :] = loss


def scale_bits(x):
    top = jnp.max(jnp.abs(x), axis=-2, keepdims=True)
    return jnp.ceil(jnp.log2(jnp.maximum(top, 1e-30)))


def to_code(x):
    return jnp.round(x).astype(jnp.int32).astype(jnp.int16)


def from_code(x):
    return x.astype(jnp.int32).astype(jnp.float32)


def join_kernel(body, per_owner, keep_ref, got_ref, after_ref, out_ref):
    del after_ref
    chunks, _, lanes = keep_ref.shape
    ends = body + 2 * per_owner
    dec = keep_ref[:, :body, :] + got_ref[:, :body, :]
    dec_bits = scale_bits(dec)
    out_ref[:, :body, :] = to_code(dec * (CODE_TOP * jnp.exp2(-dec_bits)))
    rows = slice(body, body + per_owner)
    moved = jnp.concatenate([keep_ref[:, rows, :], got_ref[:, rows, :]], axis=1)
    bits = scale_bits(moved)
    out_ref[:, body:ends, :] = to_code(moved * (CODE_TOP * jnp.exp2(-bits)))
    loss = keep_ref[:, body + per_owner :, :] + got_ref[:, body + per_owner :, :]
    loss = loss[:, :1, :]
    loss_bits = scale_bits(loss)
    loss = loss * (LOSS_TOP * jnp.exp2(-loss_bits))
    high = jnp.round(loss)
    low = (loss - high) * LOSS_TOP
    at = lax.broadcasted_iota(jnp.int32, (chunks, META, lanes), 1)
    meta = jnp.zeros((chunks, META, lanes), jnp.float32)
    for i, value in enumerate((dec_bits, bits, loss_bits, high, low)):
        meta = jnp.where(at == i, value, meta)
    out_ref[:, ends:, :] = to_code(meta)


def place_kernel(parity_ref, request_ref, after_ref, out_ref):
    del after_ref
    peers = request_ref.shape[0]
    rows = request_ref[...][:, 0, :]
    walk = [2 * turn(i, peers // 2) + side for i in range(peers // 2) for side in range(2)]
    even = jnp.concatenate([rows[d : d + 1, :] for d in walk], axis=1)
    odd = jnp.concatenate([rows[d ^ 1 : (d ^ 1) + 1, :] for d in walk], axis=1)
    wanted = jnp.where(parity_ref[0] == 0, even, odd)
    out_ref[...] = one_hot(lax.broadcasted_iota(jnp.int32, out_ref.shape, 0) == wanted)


def finish_kernel(
    body,
    per_owner,
    dec_scale,
    loss_scale,
    chosen_ref,
    got_ref,
    feat_hbm,
    dec_hbm,
    loss_hbm,
    feat,
    dec,
    loss,
    sems,
):
    chunks, _, lanes = got_ref.shape
    share = dec.shape[0]
    ends = body + 2 * per_owner
    meta = from_code(got_ref[:, ends:, :])
    moved = from_code(got_ref[:, body:ends, :]) * (jnp.exp2(meta[:, 1:2, :]) / CODE_TOP)
    high, low = split(moved.reshape(chunks * 2 * per_owner, lanes))
    blocks = sems.shape[0] - 2
    step = feat.shape[0] // blocks
    copies = []
    for i in range(blocks):
        own = slice(i * step, (i + 1) * step)
        chosen = chosen_ref[own, :]
        feat[own, :] = dot(chosen, high) + dot(chosen, low)
        span = pl.ds(i * step, step)
        copies.append(pltpu.make_async_copy(feat.at[span], feat_hbm.at[span], sems.at[i]))
        copies[-1].start()
    parts = from_code(got_ref[:, :body, :]) * jnp.exp2(meta[:, 0:1, :])
    total = jnp.sum(parts, axis=0) * (dec_scale / CODE_TOP)
    for j in range(body // share):
        dec[:, j * lanes : (j + 1) * lanes] = total[j * share : (j + 1) * share, :]
    copies.append(pltpu.make_async_copy(dec, dec_hbm, sems.at[blocks]))
    copies[-1].start()
    sums = (meta[:, 3:4, :] + meta[:, 4:5, :] * (1.0 / LOSS_TOP)) * jnp.exp2(meta[:, 2:3, :])
    loss[...] = jnp.sum(sums, axis=0) * (loss_scale / LOSS_TOP)
    copies.append(pltpu.make_async_copy(loss, loss_hbm, sems.at[blocks + 1]))
    copies[-1].start()
    for copy in copies:
        copy.wait()


def local(
    features, fetch_ids, tile_lists, depth_order, alpha_codes, list_counts, targets, dec_weight
):
    f32, bf16 = jnp.float32, jnp.bfloat16
    peers = lax.axis_size("wide")
    owned, channels = features.shape
    per_owner = fetch_ids.shape[2]
    rows = peers * per_owner
    tiles, list_len, pixels = alpha_codes.shape
    width = targets.shape[1]
    slots = tiles * list_len
    chunks = peers // 2
    share = channels // peers
    lanes = 128
    body = share * (width // lanes)
    parity = lax.rem(lax.axis_index("wide"), 2)
    shape = jax.ShapeDtypeStruct
    outgoing = pl.pallas_call(
        pick_kernel,
        out_shape=shape((rows, channels), bf16),
        in_specs=[HBM, HBM],
        out_specs=HBM,
        scratch_shapes=[
            pltpu.VMEM((peers, 1, per_owner), jnp.int32),
            pltpu.VMEM((owned, channels), bf16),
            pltpu.VMEM((rows, channels), bf16),
            pltpu.SemaphoreType.DMA((4,)),
        ],
        cost_estimate=pl.CostEstimate(
            flops=20_000_000_000, bytes_accessed=40_000_000, transcendentals=0
        ),
        compiler_params=params(16),
        name="pick",
    )(pin(fetch_ids), pin(features))
    buffer = lax.all_to_all(
        outgoing.reshape(peers, per_owner, channels), "wide", split_axis=0, concat_axis=0, tiled=True
    ).reshape(rows, channels)
    grams = pl.pallas_call(
        gram_kernel,
        out_shape=(
            shape((rows, rows), bf16),
            shape((rows, rows), bf16),
            shape((rows, width), bf16),
            shape((rows, width), bf16),
            shape((rows, channels), f32),
            shape((channels, channels), bf16),
            shape((channels, channels), bf16),
            shape((8, lanes), f32),
        ),
        in_specs=[VMEM] * 5 + [HBM],
        out_specs=(VMEM,) * 8,
        scratch_shapes=[
            pltpu.VMEM((rows, slots), bf16),
            pltpu.VMEM((rows, slots), bf16),
            pltpu.VMEM((rows, slots), bf16),
            pltpu.VMEM((slots, pixels), bf16),
            pltpu.VMEM((slots, width), bf16),
            pltpu.VMEM((slots, width), bf16),
            pltpu.VMEM((tiles * pixels, width), bf16),
            pltpu.VMEM((rows, width), f32),
            pltpu.SemaphoreType.DMA((4,)),
        ],
        cost_estimate=pl.CostEstimate(
            flops=2 * slots * pixels * width + 4 * rows * slots * (width + rows),
            bytes_accessed=targets.size * 2 + alpha_codes.size * 4,
            transcendentals=2 * alpha_codes.size,
        ),
        compiler_params=params(36),
        name="gram",
    )(*map(near, (list_counts, tile_lists, depth_order, dec_weight, alpha_codes)), pin(targets))
    half_shape = shape((chunks, body + per_owner + 8, lanes), f32)
    send, keep = pl.pallas_call(
        gradient_kernel,
        out_shape=(half_shape, half_shape),
        in_specs=[SMEM] + [VMEM] * 10,
        out_specs=(VMEM, VMEM),
        scratch_shapes=[pltpu.VMEM((rows, channels), f32)],
        compiler_params=params(24),
        name="gradient",
    )(parity.reshape(1), buffer, *grams, dec_weight)
    got = lax.ppermute(send, "wide", [(i, i ^ 1) for i in range(peers)])
    chosen = pl.pallas_call(
        place_kernel,
        out_shape=shape((owned, rows), bf16),
        in_specs=[SMEM, VMEM, ANY],
        out_specs=VMEM,
        cost_estimate=pl.CostEstimate(
            flops=owned * rows, bytes_accessed=2 * owned * rows, transcendentals=0
        ),
        compiler_params=params(32),
        name="place",
    )(parity.reshape(1), fetch_ids, send)
    joined = pl.pallas_call(
        functools.partial(join_kernel, body, per_owner),
        out_shape=shape((chunks, body + 2 * per_owner + META, lanes), jnp.int16),
        in_specs=[VMEM, VMEM, ANY],
        out_specs=VMEM,
        compiler_params=params(32),
        name="join",
    )(keep, got, chosen)
    returned = lax.all_to_all(
        joined,
        "wide",
        split_axis=0,
        concat_axis=0,
        axis_index_groups=[[2 * turn(i, chunks) + c for i in range(chunks)] for c in range(2)],
        tiled=True,
    )
    pixel_total = peers * tiles * pixels
    feat_grad, dec_grad, loss = pl.pallas_call(
        functools.partial(
            finish_kernel,
            body,
            per_owner,
            1.0 / math.sqrt(pixel_total),
            0.5 / (pixel_total * width),
        ),
        out_shape=(
            shape((owned, channels), f32),
            shape((share, width), f32),
            shape((1, lanes), f32),
        ),
        in_specs=[VMEM, VMEM],
        out_specs=(HBM,) * 3,
        scratch_shapes=[
            pltpu.VMEM((owned, channels), f32),
            pltpu.VMEM((share, width), f32),
            pltpu.VMEM((1, lanes), f32),
            pltpu.SemaphoreType.DMA((6,)),
        ],
        compiler_params=params(32),
        name="finish",
    )(chosen, returned)
    return (feat_grad, dec_grad, loss[0, :1])


def solution(mesh):
    return jax.shard_map(
        local,
        mesh=mesh,
        in_specs=(
            P(("groups", "wide"), None),
            P("groups", "wide", None),
            P(("groups", "wide"), None),
            P(("groups", "wide"), None),
            P(("groups", "wide"), None, None),
            P(("groups", "wide"), None),
            P(("groups", "wide"), None),
            P(),
        ),
        out_specs=(P(("groups", "wide"), None), P(("groups", "wide"), None), P("groups")),
        check_vma=False,
    )
```
